128 devices in a mesh: ta: 2 (over y_lo), ha: 64 (over y_hi, z, x, core).
Axes of the slice: x: 4, y: 4 (y_hi: 2, y_lo: 2; y = y_hi * 2 + y_lo), z: 4, core: 2. Of those that a mesh axis runs over, the one named last changes fastest.
Arguments:
- tokens: bfloat16 [4, 128, 10240], P(None, 'ha', 'ta'), may hold values from -6 to 6
- cache_latent: bfloat16 [2, 256, 5120], P(None, 'ha'), may hold values from -6 to 6
- cache_feature: bfloat16 [2, 512, 640, 192], P(None, 'ha'), may hold values from -0.25 to 2
- weight_in: bfloat16 [3, 3, 3, 16, 384], replicated, may hold values from -0.3125 to 0.3125
- weight_up: bfloat16 [3, 3, 384, 192], replicated, may hold values from -0.109375 to 0.109375
- weight_out: bfloat16 [3, 3, 3, 18432], replicated, may hold values from -0.078125 to 0.078125
- weight_skip: bfloat16 [192, 96], replicated, may hold values from -0.4375 to 0.4375
- bias_in: float32 [384], replicated, may hold values from -3 to 3
- bias_up: float32 [192], replicated, may hold values from -3 to 3
- bias_out: float32 [96], replicated, may hold values from -3 to 3
- gain_in: float32 [384], replicated, may hold values from 0.1 to 1.9
- gain_up: float32 [192], replicated, may hold values from 0.1 to 1.9
Outputs:
- decoded: bfloat16 [4, 512, 61440], P('ta', 'ha')
The draws below stay inside these ranges and needn't reach their ends.
All inputs are finite; a program needn't handle non-finite values.
Results may differ from the reference program's by a relative error of at most 0.0051.
Values may be sent and summed in bfloat16 or wider, within the bound.
A program may use at most 128 MiB of HBM per device.

```python
import jax
import jax.numpy as jnp
from jax import lax

C0 = 16
C1 = 384
C2 = 192
C3 = 96
WL = 320
FRAMES = 4
HL = 256
HP = 128
WP = 160
HU = 512
WU = 640


def levels(own_key, dims, split, smallest, largest):
    loudness = 1.0
    for axis_at, shards_of in split:
        heights = jax.random.uniform(jax.random.fold_in(jax.random.fold_in(own_key, 6), axis_at), (shards_of,), jnp.float32, smallest / len(split), largest / len(split))
        loudness = loudness * jnp.repeat(jnp.exp(heights), dims[axis_at] // shards_of).reshape((-1,) + (1,) * (len(dims) - 1 - axis_at))
    return loudness


def scatter_about(own_key, dims, spread, reach, shards=(), dtype=jnp.bfloat16):
    values = spread * jax.random.normal(own_key, dims, jnp.float32)
    if shards:
        values = values * levels(own_key, dims, shards, -0.22, 0.18)
    return jnp.clip(values, -reach, reach).astype(dtype)


def setup_inputs(seed: int = 0) -> dict:
    streams_of = jax.random.split(jax.random.key(seed), 13)
    tokens = scatter_about(streams_of[0], (FRAMES, HP, WP * 4 * C0), 1.0, 6.0, ((1, 64), (2, 2)))
    cache_latent = scatter_about(streams_of[1], (2, HL, WL * C0), 1.0, 6.0, ((1, 64),))
    cache_feature = jnp.clip(-0.25 + 2.25 * jax.random.uniform(streams_of[2], (2, HU, WU, C2), jnp.float32) ** levels(streams_of[2], (2, HU, WU, C2), ((1, 64),), -0.2, 0.2), -0.25, 2.0).astype(jnp.bfloat16)
    weight_in = scatter_about(streams_of[3], (3, 3, 3, C0, C1), (27 * C0) ** -0.5, 0.3125)
    weight_up = scatter_about(streams_of[4], (3, 3, C1, C2), (9 * C1) ** -0.5, 0.109375)
    weight_out = scatter_about(streams_of[5], (3, 3, 3, C2 * C3), (27 * C2) ** -0.5, 0.078125)
    weight_skip = scatter_about(streams_of[6], (C2, C3), C2 ** -0.5, 0.4375)
    bias_in = scatter_about(streams_of[7], (C1,), 0.5, 3.0, (), jnp.float32)
    bias_up = scatter_about(streams_of[8], (C2,), 0.5, 3.0, (), jnp.float32)
    bias_out = scatter_about(streams_of[9], (C3,), 0.5, 3.0, (), jnp.float32)
    gain_in = jnp.clip(1.0 + 0.18 * jax.random.normal(streams_of[10], (C1,), jnp.float32), 0.1, 1.9)
    gain_up = jnp.clip(1.0 + 0.18 * jax.random.normal(streams_of[11], (C2,), jnp.float32), 0.1, 1.9)
    return {"tokens": tokens, "cache_latent": cache_latent, "cache_feature": cache_feature, "weight_in": weight_in, "weight_up": weight_up, "weight_out": weight_out, "weight_skip": weight_skip, "bias_in": bias_in, "bias_up": bias_up, "bias_out": bias_out, "gain_in": gain_in, "gain_up": gain_up}


def normed(field, gain):
    scale = lax.rsqrt(lax.optimization_barrier(jnp.mean(field * field, axis=-1, keepdims=True)) + 1e-06)
    return jax.nn.silu(field * scale * gain.astype(jnp.float32))

def conv_time(field, kernel):
    return lax.conv_general_dilated(field[None], kernel, (1, 1, 1), [(0, 0), (1, 1), (1, 1)], dimension_numbers=('NDHWC', 'DHWIO', 'NDHWC'), precision=lax.Precision.HIGHEST)[0]

def conv_plane(field, kernel):
    return lax.conv_general_dilated(field[None], kernel, (1, 1), [(1, 1), (1, 1)], dimension_numbers=('NHWC', 'HWIO', 'NHWC'), precision=lax.Precision.HIGHEST)[0]

def reference(tokens, cache_latent, cache_feature, weight_in, weight_up, weight_out, weight_skip, bias_in, bias_up, bias_out, gain_in, gain_up):
    latent = tokens.reshape(FRAMES, HP, WP, 2, 2, C0).transpose(0, 1, 3, 2, 4, 5).reshape(FRAMES, HL, WL, C0)
    sequence = jnp.concatenate([cache_latent.reshape(2, HL, WL, C0), latent], 0).astype(jnp.float32)
    first_map = conv_time(sequence, weight_in.astype(jnp.float32)) + bias_in
    first_act = normed(first_map, gain_in).astype(jnp.bfloat16)
    kernel_up = weight_up.astype(jnp.float32)
    second_list = []
    skip_list = []
    for frame in range(FRAMES):
        lifted = jnp.repeat(jnp.repeat(first_act[frame], 2, axis=0), 2, axis=1).astype(jnp.float32)
        second_map = conv_plane(lifted, kernel_up) + bias_up
        second_list.append(normed(second_map, gain_up).astype(jnp.bfloat16))
        skip_list.append(second_map.astype(jnp.bfloat16))
    features = jnp.concatenate([cache_feature.reshape(2, HU, WU, C2), jnp.stack(second_list, 0)], 0)
    kernel_out = weight_out.reshape(3, 3, 3, C2, C3).astype(jnp.float32)
    outputs = []
    for frame in range(FRAMES):
        window = features[frame:frame + 3].astype(jnp.float32)
        main = conv_time(window, kernel_out)[0]
        skipped = jnp.dot(skip_list[frame].reshape(HU * WU, C2), weight_skip, preferred_element_type=jnp.float32).reshape(HU, WU, C3)
        outputs.append((main + bias_out + skipped).astype(jnp.bfloat16))
    return jnp.stack(outputs, 0).reshape(FRAMES, HU, WU * C3)
```

```python
import functools

import jax
import jax.numpy as jnp
from jax import lax
from jax.experimental import pallas as pl
from jax.experimental.pallas import tpu as pltpu
from jax.sharding import PartitionSpec as P

C0 = 16
C1 = 384
C2 = 192
C3 = 96
FRAMES = 4
PATCH_COLS = 80
HALO = 16
TOK = PATCH_COLS + 2 * HALO
WIDE = 96
FCOLS = 320
BF = jnp.bfloat16
F32 = jnp.float32
MESH = pl.DeviceIdType.MESH


def silu_half(half):
    return half + half * jnp.tanh(half)


def kernel(
    tokens,
    cache_lat,
    cache_feat,
    w1_hbm,
    w2_hbm,
    w3_hbm,
    b1,
    b2,
    b3,
    g1,
    g2,
    out,
    tok,
    win,
    y1,
    a_r0,
    a_r1p,
    a_r1c,
    y2e,
    y2o,
    fe,
    fo,
    fe1,
    ue,
    uo,
    cf,
    cs,
    acc,
    ostage,
    w1,
    w2,
    w3,
    send_sem,
    recv_sem,
    local_sem,
):
    ta = lax.axis_index("ta")
    ha = lax.axis_index("ha")
    n_ha = lax.axis_size("ha")
    up = lax.rem(ha + n_ha - 1, n_ha)
    down = lax.rem(ha + 1, n_ha)
    other = 1 - ta
    top = ha == 0
    bottom = ha == n_ha - 1
    left = ta == 0

    lat_src = pl.multiple_of(ta * 64, 16)
    lat_dst = pl.multiple_of(HALO - ta * HALO, 16)
    feat_src = pl.multiple_of(ta * 304, 16)
    feat_dst = pl.multiple_of(HALO - ta * HALO, 16)
    edge_src = pl.multiple_of((1 - ta) * 64, 16)
    edge_dst = pl.multiple_of(ta * 96, 16)
    local = [
        pltpu.make_async_copy(
            tokens, tok.at[2:6, 1:3, HALO : HALO + PATCH_COLS], local_sem.at[0]
        ),
        pltpu.make_async_copy(
            cache_lat.at[:, :, pl.ds(lat_src, 96)],
            tok.at[0:2, 1:3, pl.ds(lat_dst, 96)],
            local_sem.at[1],
        ),
        pltpu.make_async_copy(w1_hbm, w1, local_sem.at[2]),
        pltpu.make_async_copy(w2_hbm, w2, local_sem.at[3]),
        pltpu.make_async_copy(
            cache_feat.at[:, :, pl.ds(feat_src, 336)],
            cf.at[:, 1:9, pl.ds(feat_dst, 336)],
            local_sem.at[4],
        ),
        pltpu.make_async_copy(w3_hbm, w3, local_sem.at[5]),
    ]
    for copy in local:
        copy.start()

    barrier = pltpu.get_barrier_semaphore()
    partners = [(ta, up), (ta, down), (other, ha), (other, up), (other, down)]
    for partner in partners:
        pl.semaphore_signal(barrier, inc=1, device_id=partner, device_id_type=MESH)
    pl.semaphore_wait(barrier, len(partners))

    def remote(slot, src, dst, to):
        return pltpu.make_async_remote_copy(
            src_ref=src,
            dst_ref=dst,
            send_sem=send_sem.at[slot],
            recv_sem=recv_sem.at[slot],
            device_id=to,
            device_id_type=MESH,
        )

    own = slice(HALO, HALO + PATCH_COLS)
    early = [
        remote(0, tokens.at[:, 0], tok.at[2:6, 3, own], (ta, up)),
        remote(1, tokens.at[:, 1], tok.at[2:6, 0, own], (ta, down)),
        remote(
            2,
            tokens.at[:, :, pl.ds(edge_src, HALO)],
            tok.at[2:6, 1:3, pl.ds(edge_dst, HALO)],
            (other, ha),
        ),
        remote(
            3,
            tokens.at[:, 0, pl.ds(edge_src, HALO)],
            tok.at[2:6, 3, pl.ds(edge_dst, HALO)],
            (other, up),
        ),
        remote(
            4,
            tokens.at[:, 1, pl.ds(edge_src, HALO)],
            tok.at[2:6, 0, pl.ds(edge_dst, HALO)],
            (other, down),
        ),
        remote(
            5,
            cache_lat.at[:, 0, pl.ds(lat_src, 96)],
            tok.at[0:2, 3, pl.ds(lat_dst, 96)],
            (ta, up),
        ),
        remote(
            6,
            cache_lat.at[:, 1, pl.ds(lat_src, 96)],
            tok.at[0:2, 0, pl.ds(lat_dst, 96)],
            (ta, down),
        ),
    ]
    later = [
        remote(
            7,
            cache_feat.at[:, 0, pl.ds(feat_src, 336)],
            cf.at[:, 9, pl.ds(feat_dst, 336)],
            (ta, up),
        ),
        remote(
            8,
            cache_feat.at[:, 7, pl.ds(feat_src, 336)],
            cf.at[:, 0, pl.ds(feat_dst, 336)],
            (ta, down),
        ),
    ]
    for copy in early + later:
        copy.start()

    @pl.when(left)
    def _():
        tok[:, :, 0:HALO] = jnp.zeros((6, 4, HALO, 4 * C0), BF)
        cf[:, :, 0:HALO] = jnp.zeros((2, 10, HALO, C2), BF)

    @pl.when(jnp.logical_not(left))
    def _():
        tok[:, :, HALO + PATCH_COLS :] = jnp.zeros((6, 4, HALO, 4 * C0), BF)
        cf[:, :, HALO + FCOLS :] = jnp.zeros((2, 10, HALO, C2), BF)

    for copy in early:
        copy.wait()
    local[0].wait()
    local[1].wait()

    @pl.when(top)
    def _():
        tok[:, 0] = jnp.zeros((6, TOK, 4 * C0), BF)

    @pl.when(bottom)
    def _():
        tok[:, 3] = jnp.zeros((6, TOK, 4 * C0), BF)

    lane64 = lax.broadcasted_iota(jnp.int32, (TOK, 4 * C0), 1)
    second_row = lane64 >= 2 * C0
    second_col = (lane64 // C0) % 2 == 1

    def windows(t, carry):
        rows = [tok[t, u].astype(F32) for u in range(4)]
        for u in range(4):
            above = rows[max(u - 1, 0)]
            below = rows[min(u + 1, 3)]
            here = rows[u]
            vert = jnp.where(second_row, above, below)
            horiz = jnp.where(second_col, pltpu.roll(here, 1, 0), pltpu.roll(here, TOK - 1, 0))
            diag = jnp.where(second_col, pltpu.roll(vert, 1, 0), pltpu.roll(vert, TOK - 1, 0))
            full = jnp.concatenate([here, vert, horiz, diag], axis=1)
            win[t, u] = pltpu.roll(full, 1, 0)[HALO : HALO + WIDE].astype(BF)
        return carry

    lax.fori_loop(0, 6, windows, 0)
    local[2].wait()

    def first(row, carry):
        u = (row + 1) // 2
        q = (row + 1) % 2
        lhs = jnp.concatenate(
            [win[dt : dt + 4, u].reshape(4 * WIDE, 256) for dt in range(3)], axis=1
        )
        y1[...] = jnp.dot(lhs, w1[q], preferred_element_type=F32)

        def finish(f, inner):
            base = pl.multiple_of(f * WIDE, WIDE)
            acts = []
            for r in range(2):
                v = y1[pl.ds(base, WIDE), r * C1 : (r + 1) * C1] + b1[...]
                scale = lax.rsqrt(jnp.mean(v * v, axis=1, keepdims=True) + 1e-06)
                acts.append(silu_half(v * scale * (0.5 * g1[...])))
            a_r0[f, row] = pltpu.roll(acts[0], WIDE - 1, 0).astype(BF)
            a_r1p[f, row] = acts[1].astype(BF)
            a_r1c[f, row] = pltpu.roll(acts[1], WIDE - 1, 0)[:PATCH_COLS].astype(BF)
            return inner

        lax.fori_loop(0, 4, finish, 0)
        return carry

    lax.fori_loop(0, 6, first, 0)

    @pl.when(top)
    def _():
        a_r0[:, 0] = jnp.zeros((4, WIDE, C1), BF)
        a_r1p[:, 0] = jnp.zeros((4, WIDE, C1), BF)
        a_r1c[:, 0] = jnp.zeros((4, PATCH_COLS, C1), BF)

    @pl.when(bottom)
    def _():
        a_r0[:, 5] = jnp.zeros((4, WIDE, C1), BF)
        a_r1p[:, 5] = jnp.zeros((4, WIDE, C1), BF)
        a_r1c[:, 5] = jnp.zeros((4, PATCH_COLS, C1), BF)

    sub16 = lax.broadcasted_iota(jnp.int32, (16, 2 * C2), 0)
    lane16 = lax.broadcasted_iota(jnp.int32, (16, 2 * C2), 1)

    @pl.when(left)
    def _():
        for f in range(4):
            for row in range(6):
                kept = a_r1p[f, row, 0:16].astype(F32)
                a_r1p[f, row, 0:16] = jnp.where(sub16 == 0, 0.0, kept).astype(BF)

    @pl.when(jnp.logical_not(left))
    def _():
        a_r0[:, :, PATCH_COLS:] = jnp.zeros((4, 6, WIDE - PATCH_COLS, C1), BF)

    local[4].wait()
    for copy in later:
        copy.wait()

    @pl.when(top)
    def _():
        cf[:, 0] = jnp.zeros((2, FCOLS + 2 * HALO, C2), BF)

    @pl.when(bottom)
    def _():
        cf[:, 9] = jnp.zeros((2, FCOLS + 2 * HALO, C2), BF)

    def cached(n, carry):
        t = n // 10
        row = n % 10
        wide = cf[t, row].astype(F32)
        cs[0] = wide[:, 0:128]
        cs[1, :, 0:64] = wide[:, 128:192]

        def columns(start):
            part = pl.ds(start, PATCH_COLS, stride=4)
            return jnp.concatenate([cs[0, part, :], cs[1, part, :][:, :64]], axis=1)

        for ref, start in ((fe, 15), (fo, 17), (fe1, 19)):
            pair = jnp.concatenate([columns(start), columns(start + 1)], axis=1)
            ref[t, row] = pair.astype(BF)
        return carry

    lax.fori_loop(0, 20, cached, 0)
    local[3].wait()

    low_half = lax.broadcasted_iota(jnp.int32, (1, 128), 1) < 64

    def norm_pair(v):
        v0, v1, v2 = v[:, 0:128], v[:, 128:256], v[:, 256:384]
        sq1 = v1 * v1
        sum_a = jnp.sum(v0 * v0 + jnp.where(low_half, sq1, 0.0), axis=1, keepdims=True)
        sum_b = jnp.sum(v2 * v2 + jnp.where(low_half, 0.0, sq1), axis=1, keepdims=True)
        scale_a = lax.rsqrt(sum_a * (1.0 / C2) + 1e-06)
        scale_b = lax.rsqrt(sum_b * (1.0 / C2) + 1e-06)
        scaled = jnp.concatenate(
            [v0 * scale_a, v1 * jnp.where(low_half, scale_a, scale_b), v2 * scale_b], axis=1
        )
        return silu_half(scaled * (0.5 * g2[...]))

    first_col = lax.broadcasted_iota(jnp.int32, (1, 2 * C2), 1) < C2

    def second(f):
        lhs = jnp.concatenate(
            [a_r1p[f, 0:5], a_r0[f, 0:5], a_r1p[f, 1:6], a_r0[f, 1:6]], axis=2
        ).reshape(5 * WIDE, 4 * C1)
        y2e[...] = jnp.dot(lhs, w2[...], preferred_element_type=F32)
        lhs = jnp.concatenate(
            [a_r0[f, 0:5, :PATCH_COLS], a_r1c[f, 0:5], a_r0[f, 1:6, :PATCH_COLS], a_r1c[f, 1:6]],
            axis=2,
        ).reshape(5 * PATCH_COLS, 4 * C1)
        y2o[...] = jnp.dot(lhs, w2[...], preferred_element_type=F32)

        def finish(i, carry):
            for par in range(2):
                row = 2 * i + par
                cols = slice(par * 384, (par + 1) * 384)
                ve = y2e[pl.ds(pl.multiple_of(i * WIDE, WIDE), WIDE), cols] + b2[...]
                vo = y2o[pl.ds(pl.multiple_of(i * PATCH_COLS, 16), PATCH_COLS), cols] + b2[...]
                act = norm_pair(ve)
                fe[f + 2, row] = act[:PATCH_COLS].astype(BF)
                fe1[f + 2, row] = pltpu.roll(act, WIDE - 1, 0)[:PATCH_COLS].astype(BF)
                fo[f + 2, row] = norm_pair(vo).astype(BF)
                ve1 = pltpu.roll(ve, WIDE - 1, 0)[:PATCH_COLS]
                ue[f, row] = jnp.where(first_col, vo, ve[:PATCH_COLS]).astype(BF)
                uo[f, row] = jnp.where(first_col, ve1, vo).astype(BF)
            return carry

        lax.fori_loop(0, 5, finish, 0)

        @pl.when(top)
        def _():
            for ref in (fe, fo, fe1):
                ref[f + 2, 0] = jnp.zeros((PATCH_COLS, 2 * C2), BF)

        @pl.when(bottom)
        def _():
            for ref in (fe, fo, fe1):
                ref[f + 2, 9] = jnp.zeros((PATCH_COLS, 2 * C2), BF)

        @pl.when(left)
        def _():
            for row in range(10):
                kept = fe[f + 2, row, 0:16].astype(F32)
                gone = jnp.logical_and(sub16 == 0, lane16 < C2)
                fe[f + 2, row, 0:16] = jnp.where(gone, 0.0, kept).astype(BF)

        @pl.when(jnp.logical_not(left))
        def _():
            for row in range(10):
                kept = fe1[f + 2, row, 64:80].astype(F32)
                gone = jnp.logical_and(sub16 == 15, lane16 >= C2)
                fe1[f + 2, row, 64:80] = jnp.where(gone, 0.0, kept).astype(BF)

    def third(f):
        def rows4(n, carry):
            y = n * 4
            blocks = []
            for dt in range(3):
                for dr in range(3):
                    part = pl.ds(y + dr, 4)
                    e, o, e1 = fe[f + dt, part], fo[f + dt, part], fe1[f + dt, part]
                    blocks.append(
                        jnp.concatenate(
                            [
                                jnp.concatenate([e, o], axis=2),
                                jnp.concatenate([o, e1], axis=2),
                            ],
                            axis=0,
                        ).reshape(8 * PATCH_COLS, 768)
                    )
            mine = pl.ds(y + 1, 4)
            blocks.append(
                jnp.concatenate([ue[f, mine], uo[f, mine]], axis=0).reshape(8 * PATCH_COLS, 384)
            )
            res = jnp.dot(
                jnp.concatenate(blocks, axis=1), w3[...], preferred_element_type=F32
            )
            half = 4 * PATCH_COLS
            both = jnp.concatenate([res[:half], res[half:]], axis=1)
            for piece in range(3):
                acc[piece, pl.ds(pl.multiple_of(y * PATCH_COLS, 16), half), :] = both[
                    :, piece * 128 : (piece + 1) * 128
                ]
            return carry

        lax.fori_loop(0, 2, rows4, 0)

        def turn(s, carry):
            part = pl.ds(s, 8, stride=PATCH_COLS)
            x = jnp.concatenate([acc[piece, part, :] for piece in range(3)], axis=1) + b3[...]
            ostage[f, :, pl.ds(pl.multiple_of(s * 384, 128), 384)] = x.astype(BF)
            return carry

        lax.fori_loop(0, PATCH_COLS, turn, 0)

    for f in range(3):
        second(f)
    local[5].wait()

    half_lanes = PATCH_COLS * 384
    lanes = pl.ds(pl.multiple_of(ta * half_lanes, 128), half_lanes)

    def sent(k):
        f = 2 * other + k
        return remote(9 + k, ostage.at[f], out.at[k, :, lanes], (other, ha))

    def kept(k):
        f = 2 * ta + k
        return pltpu.make_async_copy(ostage.at[f], out.at[k, :, lanes], local_sem.at[6 + k])

    third(2 * other)
    sent(0).start()
    second(3)
    third(2 * other + 1)
    sent(1).start()
    third(2 * ta)
    kept(0).start()
    third(2 * ta + 1)
    kept(1).start()
    for k in range(2):
        kept(k).wait()
    for k in range(2):
        sent(k).wait()


def first_weight(weight_in):
    outs = []
    for q in range(2):
        cols = []
        for r in range(2):
            w = jnp.pad(weight_in, ((0, 0), (q, 1 - q), (r, 1 - r), (0, 0), (0, 0)))
            w = jnp.roll(w, (-1, -1), (1, 2)).reshape(3, 2, 2, 2, 2, C0, C1)
            cols.append(w.transpose(0, 3, 1, 2, 4, 5, 6).reshape(768, C1))
        outs.append(jnp.concatenate(cols, axis=1))
    return jnp.stack(outs)


def second_weight(weight_up):
    w = weight_up.astype(F32)

    def pick(arr, axis, k, par):
        s = functools.partial(lax.index_in_dim, arr, axis=axis, keepdims=False)
        return {
            (0, 0): lambda: s(0) + s(1),
            (1, 0): lambda: s(2),
            (0, 1): lambda: s(0),
            (1, 1): lambda: s(1) + s(2),
        }[(k, par)]()

    rows = []
    for kr in range(2):
        for kc in range(2):
            rows.append(
                jnp.concatenate(
                    [pick(pick(w, 0, kr, pr), 0, kc, pc) for pr in range(2) for pc in range(2)],
                    axis=1,
                )
            )
    return jnp.concatenate(rows, axis=0).astype(BF)


def third_weight(weight_out, weight_skip):
    w = weight_out.reshape(9, 3 * C2, C3)
    z = jnp.zeros((9, C2, C3), BF)
    main = jnp.concatenate(
        [jnp.concatenate([w, z], axis=1), jnp.concatenate([z, w], axis=1)], axis=2
    ).reshape(9 * 768, 2 * C3)
    zs = jnp.zeros((C2, C3), BF)
    skip = jnp.concatenate(
        [jnp.concatenate([zs, weight_skip], axis=1), jnp.concatenate([weight_skip, zs], axis=1)],
        axis=0,
    )
    return jnp.concatenate([main, skip], axis=0)


def shards(
    tokens,
    cache_latent,
    cache_feature,
    weight_in,
    weight_up,
    weight_out,
    weight_skip,
    bias_in,
    bias_up,
    bias_out,
    gain_in,
    gain_up,
):
    tok = tokens.reshape(4, 2, PATCH_COLS, 4 * C0)
    lat = (
        cache_latent.reshape(2, 2, 2, 160, 2, C0)
        .transpose(0, 1, 3, 2, 4, 5)
        .reshape(2, 2, 160, 4 * C0)
    )
    any_spec = pl.BlockSpec(memory_space=pl.ANY)
    vmem = pl.BlockSpec(memory_space=pltpu.VMEM)
    scratch = [
        pltpu.VMEM((6, 4, TOK, 4 * C0), BF),
        pltpu.VMEM((6, 4, WIDE, 256), BF),
        pltpu.VMEM((4 * WIDE, 2 * C1), F32),
        pltpu.VMEM((4, 6, WIDE, C1), BF),
        pltpu.VMEM((4, 6, WIDE, C1), BF),
        pltpu.VMEM((4, 6, PATCH_COLS, C1), BF),
        pltpu.VMEM((5 * WIDE, 4 * C2), F32),
        pltpu.VMEM((5 * PATCH_COLS, 4 * C2), F32),
        pltpu.VMEM((6, 10, PATCH_COLS, 2 * C2), BF),
        pltpu.VMEM((6, 10, PATCH_COLS, 2 * C2), BF),
        pltpu.VMEM((6, 10, PATCH_COLS, 2 * C2), BF),
        pltpu.VMEM((4, 10, PATCH_COLS, 2 * C2), BF),
        pltpu.VMEM((4, 10, PATCH_COLS, 2 * C2), BF),
        pltpu.VMEM((2, 10, FCOLS + 2 * HALO, C2), BF),
        pltpu.VMEM((2, FCOLS + 2 * HALO, 128), F32),
        pltpu.VMEM((3, 8 * PATCH_COLS, 128), F32),
        pltpu.VMEM((4, 8, PATCH_COLS * 384), BF),
        pltpu.VMEM((2, 768, 2 * C1), BF),
        pltpu.VMEM((4 * C1, 4 * C2), BF),
        pltpu.VMEM((9 * 768 + 384, 2 * C3), BF),
        pltpu.SemaphoreType.DMA((11,)),
        pltpu.SemaphoreType.DMA((11,)),
        pltpu.SemaphoreType.DMA((8,)),
    ]
    return pl.pallas_call(
        kernel,
        out_shape=jax.ShapeDtypeStruct((2, 8, 640 * C3), BF),
        in_specs=[any_spec] * 6 + [vmem] * 5,
        out_specs=any_spec,
        scratch_shapes=scratch,
        compiler_params=pltpu.CompilerParams(
            collective_id=0, has_side_effects=True, vmem_limit_bytes=60 * 1024 * 1024
        ),
        cost_estimate=pl.CostEstimate(
            flops=28_000_000_000, bytes_accessed=16_000_000, transcendentals=5_000_000
        ),
    )(
        tok,
        lat,
        cache_feature,
        first_weight(weight_in),
        second_weight(weight_up),
        third_weight(weight_out, weight_skip),
        bias_in.reshape(1, C1),
        jnp.tile(bias_up, 2).reshape(1, 2 * C2),
        jnp.tile(bias_out, 4).reshape(1, 4 * C3),
        gain_in.reshape(1, C1),
        jnp.tile(gain_up, 2).reshape(1, 2 * C2),
    )


def solution(mesh):
    placed = (
        P(None, "ha", "ta"),
        P(None, "ha", None),
        P(None, "ha", None, None),
        P(),
        P(),
        P(),
        P(),
        P(),
        P(),
        P(),
        P(),
        P(),
    )
    return jax.shard_map(
        shards, mesh=mesh, in_specs=placed, out_specs=P("ta", "ha", None), check_vma=False
    )
```

```python
import functools

import jax
import jax.numpy as jnp
from jax import lax
from jax.experimental import pallas as pl
from jax.experimental.pallas import tpu as pltpu
from jax.sharding import PartitionSpec as P

C0 = 16
C1 = 384
C2 = 192
C3 = 96
FRAMES = 4
PATCH_COLS = 80
HALO = 16
TOK = PATCH_COLS + 2 * HALO
WIDE = 96
FEAT = 384
BF = jnp.bfloat16
F32 = jnp.float32
MESH = pl.DeviceIdType.MESH


def silu_half(half):
    return half + half * jnp.tanh(half)


def kernel(
    tokens,
    cache_lat,
    cache_feat,
    w_in_hbm,
    w_up_hbm,
    w_out_hbm,
    w_skip,
    b1,
    b2,
    b3,
    g1,
    g2,
    out,
    tok,
    lat,
    win,
    y1a,
    y1b,
    a_r0,
    a_r1p,
    a_r1c,
    y2e,
    y2o,
    fe,
    fo,
    fe1,
    ue,
    uo,
    cf,
    cf_edge,
    pick,
    acc_a,
    acc_b,
    ostage,
    w_in,
    w_up,
    w_out,
    w1,
    w2,
    w3,
    send_sem,
    recv_sem,
    local_sem,
):
    ta = lax.axis_index("ta")
    ha = lax.axis_index("ha")
    n_ha = lax.axis_size("ha")
    up = jnp.maximum(ha - 1, 0)
    down = jnp.minimum(ha + 1, n_ha - 1)
    other = 1 - ta
    top = ha == 0
    bottom = ha == n_ha - 1
    left = ta == 0

    lat_src = pl.multiple_of(ta * 64, 16)
    lat_dst = pl.multiple_of(HALO - ta * HALO, 16)
    feat = pl.ds(pl.multiple_of(ta * 256, 128), 384)
    edge_src = pl.multiple_of((1 - ta) * 64, 16)
    edge_dst = pl.multiple_of(ta * 96, 16)
    local = [
        pltpu.make_async_copy(
            tokens, tok.at[:, 1:3, HALO : HALO + PATCH_COLS], local_sem.at[0]
        ),
        pltpu.make_async_copy(
            cache_lat.at[:, :, pl.ds(lat_src, 96)],
            lat.at[:, 2:6, pl.ds(lat_dst, 96)],
            local_sem.at[1],
        ),
        pltpu.make_async_copy(w_in_hbm, w_in, local_sem.at[2]),
        pltpu.make_async_copy(w_up_hbm, w_up, local_sem.at[3]),
        pltpu.make_async_copy(cache_feat.at[:, :, :, feat], cf, local_sem.at[4]),
        pltpu.make_async_copy(w_out_hbm, w_out, local_sem.at[5]),
    ]
    for copy in local:
        copy.start()

    barrier = pltpu.get_barrier_semaphore()

    def hello(partner):
        pl.semaphore_signal(barrier, inc=1, device_id=partner, device_id_type=MESH)

    hello((other, ha))

    @pl.when(jnp.logical_not(top))
    def _():
        hello((ta, up))
        hello((other, up))

    @pl.when(jnp.logical_not(bottom))
    def _():
        hello((ta, down))
        hello((other, down))

    def remote(slot, src, dst, to):
        return pltpu.make_async_remote_copy(
            src_ref=src,
            dst_ref=dst,
            send_sem=send_sem.at[slot],
            recv_sem=recv_sem.at[slot],
            device_id=to,
            device_id_type=MESH,
        )

    own = slice(HALO, HALO + PATCH_COLS)
    to_up = [
        remote(0, tokens.at[:, 0], tok.at[:, 3, own], (ta, up)),
        remote(
            1,
            tokens.at[:, 0, pl.ds(edge_src, HALO)],
            tok.at[:, 3, pl.ds(edge_dst, HALO)],
            (other, up),
        ),
        remote(
            2,
            cache_lat.at[:, 0:2, pl.ds(lat_src, 96)],
            lat.at[:, 6:8, pl.ds(lat_dst, 96)],
            (ta, up),
        ),
        remote(3, cache_feat.at[:, 0, :, feat], cf_edge.at[1], (ta, up)),
    ]
    to_down = [
        remote(4, tokens.at[:, 1], tok.at[:, 0, own], (ta, down)),
        remote(
            5,
            tokens.at[:, 1, pl.ds(edge_src, HALO)],
            tok.at[:, 0, pl.ds(edge_dst, HALO)],
            (other, down),
        ),
        remote(
            6,
            cache_lat.at[:, 2:4, pl.ds(lat_src, 96)],
            lat.at[:, 0:2, pl.ds(lat_dst, 96)],
            (ta, down),
        ),
        remote(7, cache_feat.at[:, 7, :, feat], cf_edge.at[0], (ta, down)),
    ]
    beside = remote(
        8,
        tokens.at[:, :, pl.ds(edge_src, HALO)],
        tok.at[:, 1:3, pl.ds(edge_dst, HALO)],
        (other, ha),
    )

    local[2].wait()

    def build_first(dt, carry):
        for block in range(16):
            row_tap = ((block >> 1 & 1) + 2 * (block >> 2 & 1) + 1) % 4
            col_tap = ((block & 1) + 2 * (block >> 3) + 1) % 4
            for q in range(2):
                for r in range(2):
                    dr, dc = row_tap - q, col_tap - r
                    if 0 <= dr < 3 and 0 <= dc < 3:
                        piece = w_in[dt, dr, dc]
                    else:
                        piece = jnp.zeros((C0, C1), BF)
                    at = pl.ds(pl.multiple_of(dt * 256 + block * C0, C0), C0)
                    w1[q, at, r * C1 : (r + 1) * C1] = piece
        return carry

    lax.fori_loop(0, 3, build_first, 0)

    partners = 5 - 2 * top.astype(jnp.int32) - 2 * bottom.astype(jnp.int32)
    pl.semaphore_wait(barrier, partners)
    beside.start()

    @pl.when(jnp.logical_not(top))
    def _():
        for copy in to_up:
            copy.start()

    @pl.when(jnp.logical_not(bottom))
    def _():
        for copy in to_down:
            copy.start()

    @pl.when(left)
    def _():
        tok[:, :, 0:HALO] = jnp.zeros((4, 4, HALO, 4 * C0), BF)
        lat[:, :, 0:HALO] = jnp.zeros((2, 8, HALO, 2 * C0), BF)

    @pl.when(jnp.logical_not(left))
    def _():
        tok[:, :, HALO + PATCH_COLS :] = jnp.zeros((4, 4, HALO, 4 * C0), BF)
        lat[:, :, HALO + PATCH_COLS :] = jnp.zeros((2, 8, HALO, 2 * C0), BF)

    lane_f = lax.broadcasted_iota(jnp.int32, (PATCH_COLS, FEAT), 1)
    sub_f = lax.broadcasted_iota(jnp.int32, (PATCH_COLS, FEAT), 0)
    for b in range(6):
        hit = lane_f == 4 * sub_f + (b - 1) + 64 * ta
        pick[b * PATCH_COLS : (b + 1) * PATCH_COLS, :] = jnp.where(hit, 1.0, 0.0).astype(BF)

    local[4].wait()

    def cached_row(t, row, columns):
        res = lax.dot_general(
            pick[...], columns, (((1,), (1,)), ((), ())), preferred_element_type=F32
        )
        for b, ref in enumerate((fe, fo, fe1)):
            at = 2 * b * PATCH_COLS
            pair = jnp.concatenate(
                [res[at : at + PATCH_COLS], res[at + PATCH_COLS : at + 2 * PATCH_COLS]], axis=1
            )
            ref[t, row] = pair.astype(BF)

    def cached_own(t, carry):
        for row in range(1, 9):
            cached_row(t, row, cf[t, row - 1])
        return carry

    lax.fori_loop(0, 2, cached_own, 0)

    local[3].wait()
    taps = {(0, 0): (0, 1), (1, 0): (2,), (0, 1): (0,), (1, 1): (1, 2)}

    def total(parts):
        return functools.reduce(lambda x, y: x + y, parts)

    for kr in range(2):
        for pr in range(2):
            rows = [
                total([w_up[dr, dc].astype(F32) for dr in taps[kr, pr]]) for dc in range(3)
            ]
            for kc in range(2):
                for pc in range(2):
                    out_at = (2 * pr + pc) * C2
                    in_at = (2 * kr + kc) * C1
                    w2[out_at : out_at + C2, in_at : in_at + C1] = total(
                        [rows[dc] for dc in taps[kc, pc]]
                    ).astype(BF)

    local[5].wait()

    z = jnp.zeros((C2, C3), BF)
    for n in range(9):
        w = w_out[n]
        w3[n * 768 : (n + 1) * 768, :] = jnp.concatenate(
            [jnp.concatenate([w, z], axis=0), jnp.concatenate([z, w], axis=0)], axis=1
        )
    ws = w_skip[...]
    w3[9 * 768 : 9 * 768 + C2, :] = jnp.concatenate([z, ws], axis=1)
    w3[9 * 768 + C2 :, :] = jnp.concatenate([ws, z], axis=1)

    bias1 = b1[...].reshape(1, C1)
    gain1 = 0.5 * g1[...].reshape(1, C1)
    bias2 = jnp.concatenate([b2[...].reshape(1, C2)] * 2, axis=1)
    gain2 = 0.5 * jnp.concatenate([g2[...].reshape(1, C2)] * 2, axis=1)
    bias3 = jnp.concatenate([b3[...].reshape(1, C3)] * 4, axis=1)

    beside.wait_recv()
    local[0].wait()
    local[1].wait()

    @pl.when(top)
    def _():
        tok[:, 0] = jnp.zeros((4, TOK, 4 * C0), BF)
        lat[:, 0:2] = jnp.zeros((2, 2, TOK, 2 * C0), BF)
        cf_edge[0] = jnp.zeros((2, C2, FEAT), BF)

    @pl.when(jnp.logical_not(top))
    def _():
        for copy in to_down[:3]:
            copy.wait_recv()

    @pl.when(bottom)
    def _():
        tok[:, 3] = jnp.zeros((4, TOK, 4 * C0), BF)
        lat[:, 6:8] = jnp.zeros((2, 2, TOK, 2 * C0), BF)
        cf_edge[1] = jnp.zeros((2, C2, FEAT), BF)

    @pl.when(jnp.logical_not(bottom))
    def _():
        for copy in to_up[:3]:
            copy.wait_recv()

    lane64 = lax.broadcasted_iota(jnp.int32, (TOK, 4 * C0), 1)
    second_row = lane64 >= 2 * C0
    second_col = (lane64 // C0) % 2 == 1

    def windows(t, rows):
        for u in range(4):
            above = rows[max(u - 1, 0)]
            below = rows[min(u + 1, 3)]
            here = rows[u]
            vert = jnp.where(second_row, above, below)
            horiz = jnp.where(second_col, pltpu.roll(here, 1, 0), pltpu.roll(here, TOK - 1, 0))
            diag = jnp.where(second_col, pltpu.roll(vert, 1, 0), pltpu.roll(vert, TOK - 1, 0))
            full = jnp.concatenate([here, vert, horiz, diag], axis=1)
            win[t, u] = pltpu.roll(full, 1, 0)[HALO : HALO + WIDE].astype(BF)

    def cached_windows(t, carry):
        rows = [lat[t, n].astype(F32) for n in range(8)]
        windows(t, [jnp.concatenate(rows[2 * u : 2 * u + 2], axis=1) for u in range(4)])
        return carry

    def token_windows(t, carry):
        windows(t + 2, [tok[t, u].astype(F32) for u in range(4)])
        return carry

    lax.fori_loop(0, 2, cached_windows, 0)
    lax.fori_loop(0, 4, token_windows, 0)
    keep_top = jnp.where(top, 0.0, 1.0)
    keep_bottom = jnp.where(bottom, 0.0, 1.0)
    sub8 = lax.broadcasted_iota(jnp.int32, (8, 2 * C2), 0)
    lane8 = lax.broadcasted_iota(jnp.int32, (8, 2 * C2), 1)
    not_left = jnp.where(jnp.logical_and(sub8 == 0, left), 0.0, 1.0)
    keep_right = jnp.where(left, 1.0, 0.0)
    out_left = jnp.where(
        jnp.logical_and(jnp.logical_and(sub8 == 0, lane8 < C2), left), 0.0, 1.0
    )
    out_right = jnp.where(
        jnp.logical_and(jnp.logical_and(sub8 == 0, lane8 >= C2), jnp.logical_not(left)), 0.0, 1.0
    )

    for row in range(6):
        u, q = (row + 1) // 2, (row + 1) % 2
        y1 = (y1a, y1b)[row % 2]
        lhs = jnp.concatenate(
            [win[dt : dt + 4, u].reshape(4 * WIDE, 256) for dt in range(3)], axis=1
        )
        y1[...] = jnp.dot(lhs, w1[q], preferred_element_type=F32)
        for f in range(4):
            acts = []
            for r in range(2):
                v = y1[f * WIDE : (f + 1) * WIDE, r * C1 : (r + 1) * C1] + bias1
                scale = lax.rsqrt(jnp.mean(v * v, axis=1, keepdims=True) + 1e-06)
                act = silu_half(v * scale * gain1)
                if row == 0:
                    act = act * keep_top
                if row == 5:
                    act = act * keep_bottom
                acts.append(act)
            shifted = pltpu.roll(acts[0], WIDE - 1, 0)
            a_r0[f, row, :PATCH_COLS] = shifted[:PATCH_COLS].astype(BF)
            a_r0[f, row, PATCH_COLS:] = (shifted[PATCH_COLS:] * keep_right).astype(BF)
            a_r1p[f, row] = jnp.concatenate([acts[1][:8] * not_left, acts[1][8:]], axis=0).astype(
                BF
            )
            a_r1c[f, row] = pltpu.roll(acts[1], WIDE - 1, 0)[:PATCH_COLS].astype(BF)

    low_half = lax.broadcasted_iota(jnp.int32, (1, 128), 1) < 64

    def norm_pair(v):
        v0, v1, v2 = v[:, 0:128], v[:, 128:256], v[:, 256:384]
        sq1 = v1 * v1
        sum_a = jnp.sum(v0 * v0 + jnp.where(low_half, sq1, 0.0), axis=1, keepdims=True)
        sum_b = jnp.sum(v2 * v2 + jnp.where(low_half, 0.0, sq1), axis=1, keepdims=True)
        scale_a = lax.rsqrt(sum_a * (1.0 / C2) + 1e-06)
        scale_b = lax.rsqrt(sum_b * (1.0 / C2) + 1e-06)
        scaled = jnp.concatenate(
            [v0 * scale_a, v1 * jnp.where(low_half, scale_a, scale_b), v2 * scale_b], axis=1
        )
        return silu_half(scaled * gain2)

    first_col = lax.broadcasted_iota(jnp.int32, (1, 2 * C2), 1) < C2

    def second(f):
        lhs = jnp.concatenate(
            [a_r1p[f, 0:5], a_r0[f, 0:5], a_r1p[f, 1:6], a_r0[f, 1:6]], axis=2
        ).reshape(5 * WIDE, 4 * C1)
        y2e[...] = lax.dot_general(
            lhs, w2[...], (((1,), (1,)), ((), ())), preferred_element_type=F32
        )
        lhs = jnp.concatenate(
            [a_r0[f, 0:5, :PATCH_COLS], a_r1c[f, 0:5], a_r0[f, 1:6, :PATCH_COLS], a_r1c[f, 1:6]],
            axis=2,
        ).reshape(5 * PATCH_COLS, 4 * C1)
        y2o[...] = lax.dot_general(
            lhs, w2[...], (((1,), (1,)), ((), ())), preferred_element_type=F32
        )

        for row in range(10):
            i, par = row // 2, row % 2
            cols = slice(par * 384, (par + 1) * 384)
            ve = y2e[i * WIDE : i * WIDE + 88, cols] + bias2
            vo = y2o[i * PATCH_COLS : (i + 1) * PATCH_COLS, cols] + bias2
            act = norm_pair(ve)
            act_o = norm_pair(vo)
            if row == 0:
                act, act_o = act * keep_top, act_o * keep_top
            if row == 9:
                act, act_o = act * keep_bottom, act_o * keep_bottom
            act = jnp.concatenate(
                [act[:8] * out_left, act[8:PATCH_COLS], act[PATCH_COLS:] * out_right], axis=0
            )
            fe[f + 2, row] = act[:PATCH_COLS].astype(BF)
            fe1[f + 2, row] = pltpu.roll(act, 87, 0)[:PATCH_COLS].astype(BF)
            fo[f + 2, row] = act_o.astype(BF)
            if 1 <= row <= 8:
                ve1 = pltpu.roll(ve, 87, 0)[:PATCH_COLS]
                ue[f, row - 1] = jnp.where(first_col, vo, ve[:PATCH_COLS]).astype(BF)
                uo[f, row - 1] = jnp.where(first_col, ve1, vo).astype(BF)

    def third(f, acc):
        for y in (0, 4):
            blocks = []
            for dt in range(3):
                for dr in range(3):
                    part = slice(y + dr, y + dr + 4)
                    e, o, e1 = fe[f + dt, part], fo[f + dt, part], fe1[f + dt, part]
                    blocks.append(
                        jnp.concatenate(
                            [
                                jnp.concatenate([e, o], axis=2),
                                jnp.concatenate([o, e1], axis=2),
                            ],
                            axis=0,
                        ).reshape(8 * PATCH_COLS, 768)
                    )
            mine = slice(y, y + 4)
            blocks.append(
                jnp.concatenate([ue[f, mine], uo[f, mine]], axis=0).reshape(8 * PATCH_COLS, 384)
            )
            res = jnp.dot(jnp.concatenate(blocks, axis=1), w3[...], preferred_element_type=F32)
            half = 4 * PATCH_COLS
            both = jnp.concatenate([res[:half], res[half:]], axis=1)
            for piece in range(3):
                acc[piece, y * PATCH_COLS : y * PATCH_COLS + half, :] = both[
                    :, piece * 128 : (piece + 1) * 128
                ]

    def turn(f, acc):
        for s in range(PATCH_COLS):
            part = pl.ds(s, 8, stride=PATCH_COLS)
            x = jnp.concatenate([acc[piece, part, :] for piece in range(3)], axis=1) + bias3
            ostage[f, :, s * 384 : (s + 1) * 384] = x.astype(BF)

    def second_loop(f, carry):
        second(f)
        return carry

    lax.fori_loop(0, 3, second_loop, 0)

    @pl.when(jnp.logical_not(top))
    def _():
        to_down[3].wait_recv()

    @pl.when(jnp.logical_not(bottom))
    def _():
        to_up[3].wait_recv()

    for t in range(2):
        cached_row(t, 0, cf_edge[0, t])
        cached_row(t, 9, cf_edge[1, t])

    half_lanes = PATCH_COLS * 384
    lanes = pl.ds(pl.multiple_of(ta * half_lanes, 128), half_lanes)

    def sent(k):
        f = 2 * other + k
        return remote(9 + k, ostage.at[f], out.at[k, :, lanes], (other, ha))

    def kept(k):
        f = 2 * ta + k
        return pltpu.make_async_copy(ostage.at[f], out.at[k, :, lanes], local_sem.at[6 + k])

    third(2 * other, acc_a)
    turn(2 * other, acc_a)
    sent(0).start()
    second(3)
    third(2 * other + 1, acc_b)
    turn(2 * other + 1, acc_b)
    sent(1).start()
    third(2 * ta, acc_a)
    turn(2 * ta, acc_a)
    kept(0).start()
    third(2 * ta + 1, acc_b)
    turn(2 * ta + 1, acc_b)
    kept(1).start()
    beside.wait_send()

    @pl.when(jnp.logical_not(top))
    def _():
        for copy in to_up:
            copy.wait_send()

    @pl.when(jnp.logical_not(bottom))
    def _():
        for copy in to_down:
            copy.wait_send()

    for k in range(2):
        kept(k).wait()
    for k in range(2):
        sent(k).wait()


def shards(
    tokens,
    cache_latent,
    cache_feature,
    weight_in,
    weight_up,
    weight_out,
    weight_skip,
    bias_in,
    bias_up,
    bias_out,
    gain_in,
    gain_up,
):
    tok = tokens.reshape(4, 2, PATCH_COLS, 4 * C0)
    lat = cache_latent.reshape(2, 4, 160, 2 * C0)
    any_spec = pl.BlockSpec(memory_space=pl.ANY)
    vmem = pl.BlockSpec(memory_space=pltpu.VMEM)
    scratch = [
        pltpu.VMEM((4, 4, TOK, 4 * C0), BF),
        pltpu.VMEM((2, 8, TOK, 2 * C0), BF),
        pltpu.VMEM((6, 4, WIDE, 256), BF),
        pltpu.VMEM((4 * WIDE, 2 * C1), F32),
        pltpu.VMEM((4 * WIDE, 2 * C1), F32),
        pltpu.VMEM((4, 6, WIDE, C1), BF),
        pltpu.VMEM((4, 6, WIDE, C1), BF),
        pltpu.VMEM((4, 6, PATCH_COLS, C1), BF),
        pltpu.VMEM((5 * WIDE, 4 * C2), F32),
        pltpu.VMEM((5 * PATCH_COLS, 4 * C2), F32),
        pltpu.VMEM((6, 10, PATCH_COLS, 2 * C2), BF),
        pltpu.VMEM((6, 10, PATCH_COLS, 2 * C2), BF),
        pltpu.VMEM((6, 10, PATCH_COLS, 2 * C2), BF),
        pltpu.VMEM((4, 8, PATCH_COLS, 2 * C2), BF),
        pltpu.VMEM((4, 8, PATCH_COLS, 2 * C2), BF),
        pltpu.VMEM((2, 8, C2, FEAT), BF),
        pltpu.VMEM((2, 2, C2, FEAT), BF),
        pltpu.VMEM((6 * PATCH_COLS, FEAT), BF),
        pltpu.VMEM((3, 8 * PATCH_COLS, 128), F32),
        pltpu.VMEM((3, 8 * PATCH_COLS, 128), F32),
        pltpu.VMEM((4, 8, PATCH_COLS * 384), BF),
        pltpu.VMEM((3, 3, 3, C0, C1), BF),
        pltpu.VMEM((3, 3, C2, C1), BF),
        pltpu.VMEM((9, 3 * C2, C3), BF),
        pltpu.VMEM((2, 768, 2 * C1), BF),
        pltpu.VMEM((4 * C2, 4 * C1), BF),
        pltpu.VMEM((9 * 768 + 384, 2 * C3), BF),
        pltpu.SemaphoreType.DMA((11,)),
        pltpu.SemaphoreType.DMA((11,)),
        pltpu.SemaphoreType.DMA((8,)),
    ]
    return pl.pallas_call(
        kernel,
        out_shape=jax.ShapeDtypeStruct((2, 8, 640 * C3), BF),
        in_specs=[any_spec] * 6 + [vmem] * 6,
        out_specs=any_spec,
        scratch_shapes=scratch,
        compiler_params=pltpu.CompilerParams(
            collective_id=0, has_side_effects=True, vmem_limit_bytes=60 * 1024 * 1024
        ),
        cost_estimate=pl.CostEstimate(
            flops=28_000_000_000, bytes_accessed=16_000_000, transcendentals=5_000_000
        ),
    )(
        tok,
        lat,
        cache_feature.transpose(0, 1, 3, 2),
        weight_in,
        weight_up.transpose(0, 1, 3, 2),
        weight_out.reshape(9, 3 * C2, C3),
        weight_skip,
        bias_in,
        bias_up,
        bias_out,
        gain_in,
        gain_up,
    )


def solution(mesh):
    placed = (
        P(None, "ha", "ta"),
        P(None, "ha", None),
        P(None, "ha", None, None),
        P(),
        P(),
        P(),
        P(),
        P(),
        P(),
        P(),
        P(),
        P(),
    )
    return jax.shard_map(
        shards, mesh=mesh, in_specs=placed, out_specs=P("ta", "ha", None), check_vma=False
    )
```

```python
import functools

import jax
import jax.numpy as jnp
from jax import lax
from jax.experimental import pallas as pl
from jax.experimental.pallas import tpu as pltpu
from jax.sharding import PartitionSpec as P

C0 = 16
C1 = 384
C2 = 192
C3 = 96
FRAMES = 4
PATCH_COLS = 80
HALO = 16
TOK = PATCH_COLS + 2 * HALO
WIDE = 96
FEAT = 384
BF = jnp.bfloat16
F32 = jnp.float32
MESH = pl.DeviceIdType.MESH


def silu_half(half):
    return half + half * jnp.tanh(half)


def kernel(
    tokens,
    cache_lat,
    cache_feat,
    w_in_hbm,
    w_up_hbm,
    w_out_hbm,
    w_skip,
    b1,
    b2,
    b3,
    g1,
    g2,
    out,
    tok,
    lat,
    win,
    y1a,
    y1b,
    a_r0,
    a_r1p,
    a_r1c,
    y2e,
    y2o,
    fe,
    fo,
    fe1,
    ue,
    uo,
    cf,
    cf_edge,
    pick,
    acc_a,
    acc_b,
    ostage,
    w_in,
    w_up,
    w_out,
    w1,
    w2,
    w3,
    send_sem,
    recv_sem,
    local_sem,
):
    ta = lax.axis_index("ta")
    ha = lax.axis_index("ha")
    n_ha = lax.axis_size("ha")
    up = jnp.maximum(ha - 1, 0)
    down = jnp.minimum(ha + 1, n_ha - 1)
    other = 1 - ta
    top = ha == 0
    bottom = ha == n_ha - 1
    left = ta == 0

    lat_src = pl.multiple_of(ta * 64, 16)
    lat_dst = pl.multiple_of(HALO - ta * HALO, 16)
    feat = pl.ds(pl.multiple_of(ta * 256, 128), 384)
    edge_src = pl.multiple_of((1 - ta) * 64, 16)
    edge_dst = pl.multiple_of(ta * 96, 16)
    local = [
        pltpu.make_async_copy(
            tokens, tok.at[:, 1:3, HALO : HALO + PATCH_COLS], local_sem.at[0]
        ),
        pltpu.make_async_copy(
            cache_lat.at[:, :, pl.ds(lat_src, 96)],
            lat.at[:, 2:6, pl.ds(lat_dst, 96)],
            local_sem.at[1],
        ),
        pltpu.make_async_copy(w_in_hbm, w_in, local_sem.at[2]),
        pltpu.make_async_copy(w_up_hbm, w_up, local_sem.at[3]),
        pltpu.make_async_copy(cache_feat.at[:, :, :, feat], cf, local_sem.at[4]),
        pltpu.make_async_copy(w_out_hbm, w_out, local_sem.at[5]),
    ]
    for copy in local:
        copy.start()

    barrier = pltpu.get_barrier_semaphore()

    def hello(partner):
        pl.semaphore_signal(barrier, inc=1, device_id=partner, device_id_type=MESH)

    hello((other, ha))

    @pl.when(jnp.logical_not(top))
    def _():
        hello((ta, up))
        hello((other, up))

    @pl.when(jnp.logical_not(bottom))
    def _():
        hello((ta, down))
        hello((other, down))

    def remote(slot, src, dst, to):
        return pltpu.make_async_remote_copy(
            src_ref=src,
            dst_ref=dst,
            send_sem=send_sem.at[slot],
            recv_sem=recv_sem.at[slot],
            device_id=to,
            device_id_type=MESH,
        )

    own = slice(HALO, HALO + PATCH_COLS)
    to_up = [
        remote(0, tokens.at[:, 0], tok.at[:, 3, own], (ta, up)),
        remote(
            1,
            tokens.at[:, 0, pl.ds(edge_src, HALO)],
            tok.at[:, 3, pl.ds(edge_dst, HALO)],
            (other, up),
        ),
        remote(
            2,
            cache_lat.at[:, 0:2, pl.ds(lat_src, 96)],
            lat.at[:, 6:8, pl.ds(lat_dst, 96)],
            (ta, up),
        ),
        remote(3, cache_feat.at[:, 0, :, feat], cf_edge.at[1], (ta, up)),
    ]
    to_down = [
        remote(4, tokens.at[:, 1], tok.at[:, 0, own], (ta, down)),
        remote(
            5,
            tokens.at[:, 1, pl.ds(edge_src, HALO)],
            tok.at[:, 0, pl.ds(edge_dst, HALO)],
            (other, down),
        ),
        remote(
            6,
            cache_lat.at[:, 2:4, pl.ds(lat_src, 96)],
            lat.at[:, 0:2, pl.ds(lat_dst, 96)],
            (ta, down),
        ),
        remote(7, cache_feat.at[:, 7, :, feat], cf_edge.at[0], (ta, down)),
    ]
    beside = remote(
        8,
        tokens.at[:, :, pl.ds(edge_src, HALO)],
        tok.at[:, 1:3, pl.ds(edge_dst, HALO)],
        (other, ha),
    )

    local[2].wait()

    def build_first(dt, carry):
        for block in range(16):
            row_tap = ((block >> 1 & 1) + 2 * (block >> 2 & 1) + 1) % 4
            col_tap = ((block & 1) + 2 * (block >> 3) + 1) % 4
            for q in range(2):
                for r in range(2):
                    dr, dc = row_tap - q, col_tap - r
                    if 0 <= dr < 3 and 0 <= dc < 3:
                        piece = w_in[dt, dr, dc]
                    else:
                        piece = jnp.zeros((C0, C1), BF)
                    at = pl.ds(pl.multiple_of(dt * 256 + block * C0, C0), C0)
                    w1[q, at, r * C1 : (r + 1) * C1] = piece
        return carry

    lax.fori_loop(0, 3, build_first, 0)

    partners = 5 - 2 * top.astype(jnp.int32) - 2 * bottom.astype(jnp.int32)
    pl.semaphore_wait(barrier, partners)
    beside.start()

    @pl.when(jnp.logical_not(top))
    def _():
        for copy in to_up:
            copy.start()

    @pl.when(jnp.logical_not(bottom))
    def _():
        for copy in to_down:
            copy.start()

    @pl.when(left)
    def _():
        tok[:, :, 0:HALO] = jnp.zeros((4, 4, HALO, 4 * C0), BF)
        lat[:, :, 0:HALO] = jnp.zeros((2, 8, HALO, 2 * C0), BF)

    @pl.when(jnp.logical_not(left))
    def _():
        tok[:, :, HALO + PATCH_COLS :] = jnp.zeros((4, 4, HALO, 4 * C0), BF)
        lat[:, :, HALO + PATCH_COLS :] = jnp.zeros((2, 8, HALO, 2 * C0), BF)

    lane_f = lax.broadcasted_iota(jnp.int32, (PATCH_COLS, FEAT), 1)
    sub_f = lax.broadcasted_iota(jnp.int32, (PATCH_COLS, FEAT), 0)
    for b in range(6):
        hit = lane_f == 4 * sub_f + (b - 1) + 64 * ta
        pick[b * PATCH_COLS : (b + 1) * PATCH_COLS, :] = jnp.where(hit, 1.0, 0.0).astype(BF)

    local[4].wait()

    def cached_row(t, row, columns):
        res = lax.dot_general(
            pick[...], columns, (((1,), (1,)), ((), ())), preferred_element_type=F32
        )
        for b, ref in enumerate((fe, fo, fe1)):
            at = 2 * b * PATCH_COLS
            pair = jnp.concatenate(
                [res[at : at + PATCH_COLS], res[at + PATCH_COLS : at + 2 * PATCH_COLS]], axis=1
            )
            ref[t, row] = pair.astype(BF)

    def cached_own(t, carry):
        for row in range(1, 9):
            cached_row(t, row, cf[t, row - 1])
        return carry

    lax.fori_loop(0, 2, cached_own, 0)

    local[3].wait()
    taps = {(0, 0): (0, 1), (1, 0): (2,), (0, 1): (0,), (1, 1): (1, 2)}

    def total(parts):
        return functools.reduce(lambda x, y: x + y, parts)

    for kr in range(2):
        for pr in range(2):
            rows = [
                total([w_up[dr, dc].astype(F32) for dr in taps[kr, pr]]) for dc in range(3)
            ]
            for kc in range(2):
                for pc in range(2):
                    out_at = (2 * pr + pc) * C2
                    in_at = (2 * kr + kc) * C1
                    w2[out_at : out_at + C2, in_at : in_at + C1] = total(
                        [rows[dc] for dc in taps[kc, pc]]
                    ).astype(BF)

    local[5].wait()

    z = jnp.zeros((C2, C3), BF)
    for n in range(9):
        w = w_out[n]
        w3[n * 768 : (n + 1) * 768, :] = jnp.concatenate(
            [jnp.concatenate([w, z], axis=0), jnp.concatenate([z, w], axis=0)], axis=1
        )
    ws = w_skip[...]
    w3[9 * 768 : 9 * 768 + C2, :] = jnp.concatenate([z, ws], axis=1)
    w3[9 * 768 + C2 :, :] = jnp.concatenate([ws, z], axis=1)

    bias1 = b1[...].reshape(1, C1)
    gain1 = 0.5 * g1[...].reshape(1, C1)
    bias2 = jnp.concatenate([b2[...].reshape(1, C2)] * 2, axis=1)
    gain2 = 0.5 * jnp.concatenate([g2[...].reshape(1, C2)] * 2, axis=1)
    bias3 = jnp.concatenate([b3[...].reshape(1, C3)] * 4, axis=1)

    beside.wait_recv()
    local[0].wait()
    local[1].wait()

    lane64 = lax.broadcasted_iota(jnp.int32, (TOK, 4 * C0), 1)
    second_row = lane64 >= 2 * C0
    second_col = (lane64 // C0) % 2 == 1

    def windows(t, rows, which):
        for u in which:
            above = rows[max(u - 1, 0)]
            below = rows[min(u + 1, 3)]
            here = rows[u]
            vert = jnp.where(second_row, above, below)
            horiz = jnp.where(second_col, pltpu.roll(here, 1, 0), pltpu.roll(here, TOK - 1, 0))
            diag = jnp.where(second_col, pltpu.roll(vert, 1, 0), pltpu.roll(vert, TOK - 1, 0))
            full = jnp.concatenate([here, vert, horiz, diag], axis=1)
            win[t, u] = pltpu.roll(full, 1, 0)[HALO : HALO + WIDE].astype(BF)

    def cached_rows(t, u):
        return jnp.concatenate(
            [lat[t, 2 * u].astype(F32), lat[t, 2 * u + 1].astype(F32)], axis=1
        )

    def token_rows(t, u):
        return tok[t, u].astype(F32)

    def inner_windows(t, get, base):
        first, last = get(t, 1), get(t, 2)
        windows(t + base, [first, first, last, last], (1, 2))

    def all_windows(t, get, base):
        windows(t + base, [get(t, u) for u in range(4)], range(4))

    def each_frame(work):
        def cached_frame(t, carry):
            work(t, cached_rows, 0)
            return carry

        def token_frame(t, carry):
            work(t, token_rows, 2)
            return carry

        lax.fori_loop(0, 2, cached_frame, 0)
        lax.fori_loop(0, 4, token_frame, 0)

    keep_top = jnp.where(top, 0.0, 1.0)
    keep_bottom = jnp.where(bottom, 0.0, 1.0)
    sub8 = lax.broadcasted_iota(jnp.int32, (8, 2 * C2), 0)
    lane8 = lax.broadcasted_iota(jnp.int32, (8, 2 * C2), 1)
    not_left = jnp.where(jnp.logical_and(sub8 == 0, left), 0.0, 1.0)
    keep_right = jnp.where(left, 1.0, 0.0)
    out_left = jnp.where(
        jnp.logical_and(jnp.logical_and(sub8 == 0, lane8 < C2), left), 0.0, 1.0
    )
    out_right = jnp.where(
        jnp.logical_and(jnp.logical_and(sub8 == 0, lane8 >= C2), jnp.logical_not(left)), 0.0, 1.0
    )

    def first(row):
        u, q = (row + 1) // 2, (row + 1) % 2
        y1 = (y1a, y1b)[row % 2]
        lhs = jnp.concatenate(
            [win[dt : dt + 4, u].reshape(4 * WIDE, 256) for dt in range(3)], axis=1
        )
        y1[...] = jnp.dot(lhs, w1[q], preferred_element_type=F32)
        for f in range(4):
            acts = []
            for r in range(2):
                v = y1[f * WIDE : (f + 1) * WIDE, r * C1 : (r + 1) * C1] + bias1
                scale = lax.rsqrt(jnp.mean(v * v, axis=1, keepdims=True) + 1e-06)
                act = silu_half(v * scale * gain1)
                if row == 0:
                    act = act * keep_top
                if row == 5:
                    act = act * keep_bottom
                acts.append(act)
            shifted = pltpu.roll(acts[0], WIDE - 1, 0)
            a_r0[f, row, :PATCH_COLS] = shifted[:PATCH_COLS].astype(BF)
            a_r0[f, row, PATCH_COLS:] = (shifted[PATCH_COLS:] * keep_right).astype(BF)
            a_r1p[f, row] = jnp.concatenate([acts[1][:8] * not_left, acts[1][8:]], axis=0).astype(
                BF
            )
            a_r1c[f, row] = pltpu.roll(acts[1], WIDE - 1, 0)[:PATCH_COLS].astype(BF)

    low_half = lax.broadcasted_iota(jnp.int32, (1, 128), 1) < 64

    def norm_pair(v):
        v0, v1, v2 = v[:, 0:128], v[:, 128:256], v[:, 256:384]
        sq1 = v1 * v1
        sum_a = jnp.sum(v0 * v0 + jnp.where(low_half, sq1, 0.0), axis=1, keepdims=True)
        sum_b = jnp.sum(v2 * v2 + jnp.where(low_half, 0.0, sq1), axis=1, keepdims=True)
        scale_a = lax.rsqrt(sum_a * (1.0 / C2) + 1e-06)
        scale_b = lax.rsqrt(sum_b * (1.0 / C2) + 1e-06)
        scaled = jnp.concatenate(
            [v0 * scale_a, v1 * jnp.where(low_half, scale_a, scale_b), v2 * scale_b], axis=1
        )
        return silu_half(scaled * gain2)

    first_col = lax.broadcasted_iota(jnp.int32, (1, 2 * C2), 1) < C2

    def second_products(at_f, spans, even_rows, odd_rows):
        def window(refs, stop):
            parts = []
            for lo, hi in spans:
                pieces = [ref[at_f, lo + down : hi + down, 0:stop] for down in (0, 1) for ref in refs]
                parts.append(jnp.concatenate(pieces, axis=-1).reshape(-1, 4 * C1))
            return jnp.concatenate(parts, axis=0)

        for rows, refs, y2, stop in (
            (even_rows, (a_r1p, a_r0), y2e, WIDE),
            (odd_rows, (a_r0, a_r1c), y2o, PATCH_COLS),
        ):
            y2[0:rows] = lax.dot_general(
                window(refs, stop), w2[...], (((1,), (1,)), ((), ())), preferred_element_type=F32
            )

    def second_finish(f, i, at):
        for par in range(2):
            row = 2 * i + par
            cols = slice(par * 384, (par + 1) * 384)
            ve = y2e[at * WIDE : at * WIDE + 88, cols] + bias2
            vo = y2o[at * PATCH_COLS : (at + 1) * PATCH_COLS, cols] + bias2
            act = norm_pair(ve)
            act_o = norm_pair(vo)
            if row == 0:
                act, act_o = act * keep_top, act_o * keep_top
            if row == 9:
                act, act_o = act * keep_bottom, act_o * keep_bottom
            act = jnp.concatenate(
                [act[:8] * out_left, act[8:PATCH_COLS], act[PATCH_COLS:] * out_right], axis=0
            )
            fe[f + 2, row] = act[:PATCH_COLS].astype(BF)
            fe1[f + 2, row] = pltpu.roll(act, 87, 0)[:PATCH_COLS].astype(BF)
            fo[f + 2, row] = act_o.astype(BF)
            if 1 <= row <= 8:
                ve1 = pltpu.roll(ve, 87, 0)[:PATCH_COLS]
                ue[f, row - 1] = jnp.where(first_col, vo, ve[:PATCH_COLS]).astype(BF)
                uo[f, row - 1] = jnp.where(first_col, ve1, vo).astype(BF)

    def second(f):
        second_products(f, ((0, 2), (3, 5)), 4 * WIDE, 4 * PATCH_COLS)
        for at, i in enumerate((0, 1, 3, 4)):
            second_finish(f, i, at)

    each_frame(inner_windows)
    first(2)
    first(3)
    second_products(slice(0, 4), ((2, 3),), 4 * WIDE, 4 * PATCH_COLS)
    for f in range(4):
        second_finish(f, 2, f)

    @pl.when(top)
    def _():
        tok[:, 0] = jnp.zeros((4, TOK, 4 * C0), BF)
        lat[:, 0:2] = jnp.zeros((2, 2, TOK, 2 * C0), BF)
        cf_edge[0] = jnp.zeros((2, C2, FEAT), BF)

    @pl.when(jnp.logical_not(top))
    def _():
        for copy in to_down[:3]:
            copy.wait_recv()

    @pl.when(bottom)
    def _():
        tok[:, 3] = jnp.zeros((4, TOK, 4 * C0), BF)
        lat[:, 6:8] = jnp.zeros((2, 2, TOK, 2 * C0), BF)
        cf_edge[1] = jnp.zeros((2, C2, FEAT), BF)

    @pl.when(jnp.logical_not(bottom))
    def _():
        for copy in to_up[:3]:
            copy.wait_recv()

    each_frame(all_windows)
    for row in (0, 1, 4, 5):
        first(row)

    def third(f, start, n, acc):
        at = slice(start, start + n)
        for y in (0, 4):
            parts = []
            for dt in range(3):
                for dr in range(3):
                    rows = slice(y + dr, y + dr + 4)
                    e, o, e1 = fe[f + dt, rows, at], fo[f + dt, rows, at], fe1[f + dt, rows, at]
                    parts.append(
                        jnp.concatenate(
                            [jnp.concatenate([e, o], axis=2), jnp.concatenate([o, e1], axis=2)],
                            axis=0,
                        ).reshape(8 * n, 768)
                    )
            mine = slice(y, y + 4)
            parts.append(
                jnp.concatenate([ue[f, mine, at], uo[f, mine, at]], axis=0).reshape(8 * n, 384)
            )
            res = jnp.dot(jnp.concatenate(parts, axis=1), w3[...], preferred_element_type=F32)
            both = jnp.concatenate([res[: 4 * n], res[4 * n :]], axis=1)
            for piece in range(3):
                acc[piece, y * n : (y + 4) * n, :] = both[:, piece * 128 : (piece + 1) * 128]
        for s in range(n):
            part = pl.ds(s, 8, stride=n)
            x = jnp.concatenate([acc[piece, part, :] for piece in range(3)], axis=1) + bias3
            ostage[f, :, (start + s) * 384 : (start + s + 1) * 384] = x.astype(BF)

    def second_loop(f, carry):
        second(f)
        return carry

    lax.fori_loop(0, 3, second_loop, 0)

    @pl.when(jnp.logical_not(top))
    def _():
        to_down[3].wait_recv()

    @pl.when(jnp.logical_not(bottom))
    def _():
        to_up[3].wait_recv()

    for t in range(2):
        cached_row(t, 0, cf_edge[0, t])
        cached_row(t, 9, cf_edge[1, t])

    half_lanes = PATCH_COLS * 384
    lanes = pl.ds(pl.multiple_of(ta * half_lanes, 128), half_lanes)

    def sent(slot, k, start, n):
        f = 2 * other + k
        there = pl.ds(pl.multiple_of(ta * half_lanes + start * 384, 128), n * 384)
        return remote(
            slot,
            ostage.at[f, :, start * 384 : (start + n) * 384],
            out.at[k, :, there],
            (other, ha),
        )

    sends = [sent(9, 0, 0, 48), sent(10, 0, 48, 32), sent(11, 1, 0, PATCH_COLS)]

    def kept(k):
        f = 2 * ta + k
        return pltpu.make_async_copy(ostage.at[f], out.at[k, :, lanes], local_sem.at[6 + k])

    third(2 * other, 0, 48, acc_a)
    sends[0].start()
    third(2 * other, 48, 32, acc_b)
    sends[1].start()
    second(3)
    third(2 * other + 1, 0, PATCH_COLS, acc_a)
    sends[2].start()
    third(2 * ta, 0, PATCH_COLS, acc_b)
    kept(0).start()
    third(2 * ta + 1, 0, PATCH_COLS, acc_a)
    kept(1).start()
    beside.wait_send()

    @pl.when(jnp.logical_not(top))
    def _():
        for copy in to_up:
            copy.wait_send()

    @pl.when(jnp.logical_not(bottom))
    def _():
        for copy in to_down:
            copy.wait_send()

    for k in range(2):
        kept(k).wait()
    for copy in sends:
        copy.wait()


def copied(x):
    def body(src, dst, buf, sem_in, sem_out):
        size = 15360
        into, back = [], []
        for k in range(2):
            for n in range(4):
                at = slice(n * size, (n + 1) * size)
                into.append(pltpu.make_async_copy(src.at[k, :, at], buf.at[k, :, at], sem_in.at[k, n]))
                back.append(pltpu.make_async_copy(buf.at[k, :, at], dst.at[k, :, at], sem_out.at[k, n]))
        for copy in into:
            copy.start()
        for copy, after in zip(into, back):
            copy.wait()
            after.start()
        for copy in back:
            copy.wait()

    spec = pl.BlockSpec(memory_space=pl.ANY)
    return pl.pallas_call(
        body,
        out_shape=jax.ShapeDtypeStruct(x.shape, x.dtype),
        in_specs=[spec],
        out_specs=spec,
        scratch_shapes=[
            pltpu.VMEM(x.shape, BF),
            pltpu.SemaphoreType.DMA((2, 4)),
            pltpu.SemaphoreType.DMA((2, 4)),
        ],
    )(x)


def shards(
    tokens,
    cache_latent,
    cache_feature,
    weight_in,
    weight_up,
    weight_out,
    weight_skip,
    bias_in,
    bias_up,
    bias_out,
    gain_in,
    gain_up,
):
    tok = tokens.reshape(4, 2, PATCH_COLS, 4 * C0)
    lat = cache_latent.reshape(2, 4, 160, 2 * C0)
    any_spec = pl.BlockSpec(memory_space=pl.ANY)
    vmem = pl.BlockSpec(memory_space=pltpu.VMEM)
    scratch = [
        pltpu.VMEM((4, 4, TOK, 4 * C0), BF),
        pltpu.VMEM((2, 8, TOK, 2 * C0), BF),
        pltpu.VMEM((6, 4, WIDE, 256), BF),
        pltpu.VMEM((4 * WIDE, 2 * C1), F32),
        pltpu.VMEM((4 * WIDE, 2 * C1), F32),
        pltpu.VMEM((4, 6, WIDE, C1), BF),
        pltpu.VMEM((4, 6, WIDE, C1), BF),
        pltpu.VMEM((4, 6, PATCH_COLS, C1), BF),
        pltpu.VMEM((5 * WIDE, 4 * C2), F32),
        pltpu.VMEM((5 * PATCH_COLS, 4 * C2), F32),
        pltpu.VMEM((6, 10, PATCH_COLS, 2 * C2), BF),
        pltpu.VMEM((6, 10, PATCH_COLS, 2 * C2), BF),
        pltpu.VMEM((6, 10, PATCH_COLS, 2 * C2), BF),
        pltpu.VMEM((4, 8, PATCH_COLS, 2 * C2), BF),
        pltpu.VMEM((4, 8, PATCH_COLS, 2 * C2), BF),
        pltpu.VMEM((2, 8, C2, FEAT), BF),
        pltpu.VMEM((2, 2, C2, FEAT), BF),
        pltpu.VMEM((6 * PATCH_COLS, FEAT), BF),
        pltpu.VMEM((3, 8 * PATCH_COLS, 128), F32),
        pltpu.VMEM((3, 8 * PATCH_COLS, 128), F32),
        pltpu.VMEM((4, 8, PATCH_COLS * 384), BF),
        pltpu.VMEM((3, 3, 3, C0, C1), BF),
        pltpu.VMEM((3, 3, C2, C1), BF),
        pltpu.VMEM((9, 3 * C2, C3), BF),
        pltpu.VMEM((2, 768, 2 * C1), BF),
        pltpu.VMEM((4 * C2, 4 * C1), BF),
        pltpu.VMEM((9 * 768 + 384, 2 * C3), BF),
        pltpu.SemaphoreType.DMA((12,)),
        pltpu.SemaphoreType.DMA((12,)),
        pltpu.SemaphoreType.DMA((8,)),
    ]
    return copied(pl.pallas_call(
        kernel,
        out_shape=jax.ShapeDtypeStruct((2, 8, 640 * C3), BF),
        in_specs=[any_spec] * 6 + [vmem] * 6,
        out_specs=any_spec,
        scratch_shapes=scratch,
        compiler_params=pltpu.CompilerParams(
            collective_id=0, has_side_effects=True, vmem_limit_bytes=52 * 1024 * 1024
        ),
        cost_estimate=pl.CostEstimate(
            flops=28_000_000_000, bytes_accessed=16_000_000, transcendentals=5_000_000
        ),
    )(
        tok,
        lat,
        cache_feature.transpose(0, 1, 3, 2),
        weight_in,
        weight_up.transpose(0, 1, 3, 2),
        weight_out.reshape(9, 3 * C2, C3),
        weight_skip,
        bias_in,
        bias_up,
        bias_out,
        gain_in,
        gain_up,
    ))


def solution(mesh):
    placed = (
        P(None, "ha", "ta"),
        P(None, "ha", None),
        P(None, "ha", None, None),
        P(),
        P(),
        P(),
        P(),
        P(),
        P(),
        P(),
        P(),
        P(),
    )
    return jax.shard_map(
        shards, mesh=mesh, in_specs=placed, out_specs=P("ta", "ha", None), check_vma=False
    )
```

```python
import functools

import jax
import jax.numpy as jnp
from jax import lax
from jax.experimental import pallas as pl
from jax.experimental.pallas import tpu as pltpu
from jax.sharding import PartitionSpec as P

C0 = 16
C1 = 384
C2 = 192
C3 = 96
FRAMES = 4
PATCH_COLS = 80
HALO = 16
TOK = PATCH_COLS + 2 * HALO
WIDE = 96
FEAT = 384
BF = jnp.bfloat16
F32 = jnp.float32
MESH = pl.DeviceIdType.MESH


def silu_half(half):
    return half + half * jnp.tanh(half)


def kernel(
    tokens,
    cache_lat,
    cache_feat,
    w_in_hbm,
    w_up_hbm,
    w_out_hbm,
    w_skip,
    b1,
    b2,
    b3,
    g1,
    g2,
    out,
    tok,
    lat,
    win,
    y1a,
    y1b,
    a_r0,
    a_r1p,
    a_r1c,
    y2e,
    y2o,
    fe,
    fo,
    fe1,
    ue,
    uo,
    cf,
    cf_edge,
    pick,
    acc_a,
    acc_b,
    ostage,
    w_in,
    w_up,
    w_out,
    w1,
    w2,
    w3,
    send_sem,
    recv_sem,
    local_sem,
):
    ta = lax.axis_index("ta")
    ha = lax.axis_index("ha")
    n_ha = lax.axis_size("ha")
    up = jnp.maximum(ha - 1, 0)
    down = jnp.minimum(ha + 1, n_ha - 1)
    other = 1 - ta
    top = ha == 0
    bottom = ha == n_ha - 1
    left = ta == 0

    lat_src = pl.multiple_of(ta * 64, 16)
    lat_dst = pl.multiple_of(HALO - ta * HALO, 16)
    feat = pl.ds(pl.multiple_of(ta * 256, 128), 384)
    edge_src = pl.multiple_of((1 - ta) * 64, 16)
    edge_dst = pl.multiple_of(ta * 96, 16)
    local = [
        pltpu.make_async_copy(
            tokens, tok.at[:, 1:3, HALO : HALO + PATCH_COLS], local_sem.at[0]
        ),
        pltpu.make_async_copy(
            cache_lat.at[:, :, pl.ds(lat_src, 96)],
            lat.at[:, 2:6, pl.ds(lat_dst, 96)],
            local_sem.at[1],
        ),
        pltpu.make_async_copy(w_in_hbm, w_in, local_sem.at[2]),
        pltpu.make_async_copy(w_up_hbm, w_up, local_sem.at[3]),
        pltpu.make_async_copy(cache_feat.at[:, :, :, feat], cf, local_sem.at[4]),
        pltpu.make_async_copy(w_out_hbm, w_out, local_sem.at[5]),
    ]
    for copy in local:
        copy.start()

    barrier = pltpu.get_barrier_semaphore()

    def hello(partner):
        pl.semaphore_signal(barrier, inc=1, device_id=partner, device_id_type=MESH)

    hello((other, ha))

    @pl.when(jnp.logical_not(top))
    def _():
        hello((ta, up))
        hello((other, up))

    @pl.when(jnp.logical_not(bottom))
    def _():
        hello((ta, down))
        hello((other, down))

    def remote(slot, src, dst, to):
        return pltpu.make_async_remote_copy(
            src_ref=src,
            dst_ref=dst,
            send_sem=send_sem.at[slot],
            recv_sem=recv_sem.at[slot],
            device_id=to,
            device_id_type=MESH,
        )

    own = slice(HALO, HALO + PATCH_COLS)
    to_up = [
        remote(0, tokens.at[:, 0], tok.at[:, 3, own], (ta, up)),
        remote(
            1,
            tokens.at[:, 0, pl.ds(edge_src, HALO)],
            tok.at[:, 3, pl.ds(edge_dst, HALO)],
            (other, up),
        ),
        remote(
            2,
            cache_lat.at[:, 0:2, pl.ds(lat_src, 96)],
            lat.at[:, 6:8, pl.ds(lat_dst, 96)],
            (ta, up),
        ),
        remote(3, cache_feat.at[:, 0, :, feat], cf_edge.at[1], (ta, up)),
    ]
    to_down = [
        remote(4, tokens.at[:, 1], tok.at[:, 0, own], (ta, down)),
        remote(
            5,
            tokens.at[:, 1, pl.ds(edge_src, HALO)],
            tok.at[:, 0, pl.ds(edge_dst, HALO)],
            (other, down),
        ),
        remote(
            6,
            cache_lat.at[:, 2:4, pl.ds(lat_src, 96)],
            lat.at[:, 0:2, pl.ds(lat_dst, 96)],
            (ta, down),
        ),
        remote(7, cache_feat.at[:, 7, :, feat], cf_edge.at[0], (ta, down)),
    ]
    beside = remote(
        8,
        tokens.at[:, :, pl.ds(edge_src, HALO)],
        tok.at[:, 1:3, pl.ds(edge_dst, HALO)],
        (other, ha),
    )

    local[2].wait()

    def build_first(dt, carry):
        for block in range(16):
            row_tap = ((block >> 1 & 1) + 2 * (block >> 2 & 1) + 1) % 4
            col_tap = ((block & 1) + 2 * (block >> 3) + 1) % 4
            for q in range(2):
                for r in range(2):
                    dr, dc = row_tap - q, col_tap - r
                    if 0 <= dr < 3 and 0 <= dc < 3:
                        piece = w_in[dt, dr, dc]
                    else:
                        piece = jnp.zeros((C0, C1), BF)
                    at = pl.ds(pl.multiple_of(dt * 256 + block * C0, C0), C0)
                    w1[q, at, r * C1 : (r + 1) * C1] = piece
        return carry

    lax.fori_loop(0, 3, build_first, 0)

    partners = 5 - 2 * top.astype(jnp.int32) - 2 * bottom.astype(jnp.int32)
    pl.semaphore_wait(barrier, partners)
    beside.start()

    @pl.when(jnp.logical_not(top))
    def _():
        for copy in to_up:
            copy.start()

    @pl.when(jnp.logical_not(bottom))
    def _():
        for copy in to_down:
            copy.start()

    @pl.when(left)
    def _():
        tok[:, :, 0:HALO] = jnp.zeros((4, 4, HALO, 4 * C0), BF)
        lat[:, :, 0:HALO] = jnp.zeros((2, 8, HALO, 2 * C0), BF)

    @pl.when(jnp.logical_not(left))
    def _():
        tok[:, :, HALO + PATCH_COLS :] = jnp.zeros((4, 4, HALO, 4 * C0), BF)
        lat[:, :, HALO + PATCH_COLS :] = jnp.zeros((2, 8, HALO, 2 * C0), BF)

    lane_f = lax.broadcasted_iota(jnp.int32, (PATCH_COLS, FEAT), 1)
    sub_f = lax.broadcasted_iota(jnp.int32, (PATCH_COLS, FEAT), 0)
    for b in range(6):
        hit = lane_f == 4 * sub_f + (b - 1) + 64 * ta
        pick[b * PATCH_COLS : (b + 1) * PATCH_COLS, :] = jnp.where(hit, 1.0, 0.0).astype(BF)

    local[4].wait()

    def cached_row(t, row, columns):
        res = lax.dot_general(
            pick[...], columns, (((1,), (1,)), ((), ())), preferred_element_type=F32
        )
        for b, ref in enumerate((fe, fo, fe1)):
            at = 2 * b * PATCH_COLS
            pair = jnp.concatenate(
                [res[at : at + PATCH_COLS], res[at + PATCH_COLS : at + 2 * PATCH_COLS]], axis=1
            )
            ref[t, row] = pair.astype(BF)

    def cached_own(t, carry):
        for row in range(1, 9):
            cached_row(t, row, cf[t, row - 1])
        return carry

    lax.fori_loop(0, 2, cached_own, 0)

    local[3].wait()
    taps = {(0, 0): (0, 1), (1, 0): (2,), (0, 1): (0,), (1, 1): (1, 2)}

    def total(parts):
        return functools.reduce(lambda x, y: x + y, parts)

    for kr in range(2):
        for pr in range(2):
            rows = [
                total([w_up[dr, dc].astype(F32) for dr in taps[kr, pr]]) for dc in range(3)
            ]
            for kc in range(2):
                for pc in range(2):
                    out_at = (2 * pr + pc) * C2
                    in_at = (2 * kr + kc) * C1
                    w2[out_at : out_at + C2, in_at : in_at + C1] = total(
                        [rows[dc] for dc in taps[kc, pc]]
                    ).astype(BF)

    local[5].wait()

    z = jnp.zeros((C2, C3), BF)
    for n in range(9):
        w = w_out[n]
        w3[n * 768 : (n + 1) * 768, :] = jnp.concatenate(
            [jnp.concatenate([w, z], axis=0), jnp.concatenate([z, w], axis=0)], axis=1
        )
    ws = w_skip[...]
    w3[9 * 768 : 9 * 768 + C2, :] = jnp.concatenate([z, ws], axis=1)
    w3[9 * 768 + C2 :, :] = jnp.concatenate([ws, z], axis=1)

    bias1 = b1[...].reshape(1, C1)
    gain1 = 0.5 * g1[...].reshape(1, C1)
    bias2 = jnp.concatenate([b2[...].reshape(1, C2)] * 2, axis=1)
    gain2 = 0.5 * jnp.concatenate([g2[...].reshape(1, C2)] * 2, axis=1)
    bias3 = jnp.concatenate([b3[...].reshape(1, C3)] * 4, axis=1)

    beside.wait_recv()
    local[0].wait()
    local[1].wait()

    lane64 = lax.broadcasted_iota(jnp.int32, (TOK, 4 * C0), 1)
    second_row = lane64 >= 2 * C0
    second_col = (lane64 // C0) % 2 == 1

    def windows(t, rows, which):
        for u in which:
            above = rows[max(u - 1, 0)]
            below = rows[min(u + 1, 3)]
            here = rows[u]
            vert = jnp.where(second_row, above, below)
            horiz = jnp.where(second_col, pltpu.roll(here, 1, 0), pltpu.roll(here, TOK - 1, 0))
            diag = jnp.where(second_col, pltpu.roll(vert, 1, 0), pltpu.roll(vert, TOK - 1, 0))
            full = jnp.concatenate([here, vert, horiz, diag], axis=1)
            win[t, u] = pltpu.roll(full, 1, 0)[HALO : HALO + WIDE].astype(BF)

    def cached_rows(t, u):
        return jnp.concatenate(
            [lat[t, 2 * u].astype(F32), lat[t, 2 * u + 1].astype(F32)], axis=1
        )

    def token_rows(t, u):
        return tok[t, u].astype(F32)

    def inner_windows(t, get, base):
        first, last = get(t, 1), get(t, 2)
        windows(t + base, [first, first, last, last], (1, 2))

    def all_windows(t, get, base):
        windows(t + base, [get(t, u) for u in range(4)], range(4))

    def each_frame(work):
        def cached_frame(t, carry):
            work(t, cached_rows, 0)
            return carry

        def token_frame(t, carry):
            work(t, token_rows, 2)
            return carry

        lax.fori_loop(0, 2, cached_frame, 0)
        lax.fori_loop(0, 4, token_frame, 0)

    keep_top = jnp.where(top, 0.0, 1.0)
    keep_bottom = jnp.where(bottom, 0.0, 1.0)
    sub8 = lax.broadcasted_iota(jnp.int32, (8, 2 * C2), 0)
    lane8 = lax.broadcasted_iota(jnp.int32, (8, 2 * C2), 1)
    not_left = jnp.where(jnp.logical_and(sub8 == 0, left), 0.0, 1.0)
    keep_right = jnp.where(left, 1.0, 0.0)
    out_left = jnp.where(
        jnp.logical_and(jnp.logical_and(sub8 == 0, lane8 < C2), left), 0.0, 1.0
    )
    out_right = jnp.where(
        jnp.logical_and(jnp.logical_and(sub8 == 0, lane8 >= C2), jnp.logical_not(left)), 0.0, 1.0
    )

    def first(row):
        u, q = (row + 1) // 2, (row + 1) % 2
        y1 = (y1a, y1b)[row % 2]
        lhs = jnp.concatenate(
            [win[dt : dt + 4, u].reshape(4 * WIDE, 256) for dt in range(3)], axis=1
        )
        y1[...] = jnp.dot(lhs, w1[q], preferred_element_type=F32)
        for f in range(4):
            acts = []
            for r in range(2):
                v = y1[f * WIDE : (f + 1) * WIDE, r * C1 : (r + 1) * C1] + bias1
                scale = lax.rsqrt(jnp.mean(v * v, axis=1, keepdims=True) + 1e-06)
                act = silu_half(v * scale * gain1)
                if row == 0:
                    act = act * keep_top
                if row == 5:
                    act = act * keep_bottom
                acts.append(act)
            shifted = pltpu.roll(acts[0], WIDE - 1, 0)
            a_r0[f, row, :PATCH_COLS] = shifted[:PATCH_COLS].astype(BF)
            a_r0[f, row, PATCH_COLS:] = (shifted[PATCH_COLS:] * keep_right).astype(BF)
            a_r1p[f, row] = jnp.concatenate([acts[1][:8] * not_left, acts[1][8:]], axis=0).astype(
                BF
            )
            a_r1c[f, row] = pltpu.roll(acts[1], WIDE - 1, 0)[:PATCH_COLS].astype(BF)

    low_half = lax.broadcasted_iota(jnp.int32, (1, 128), 1) < 64

    def norm_pair(v):
        v0, v1, v2 = v[:, 0:128], v[:, 128:256], v[:, 256:384]
        sq1 = v1 * v1
        sum_a = jnp.sum(v0 * v0 + jnp.where(low_half, sq1, 0.0), axis=1, keepdims=True)
        sum_b = jnp.sum(v2 * v2 + jnp.where(low_half, 0.0, sq1), axis=1, keepdims=True)
        scale_a = lax.rsqrt(sum_a * (1.0 / C2) + 1e-06)
        scale_b = lax.rsqrt(sum_b * (1.0 / C2) + 1e-06)
        scaled = jnp.concatenate(
            [v0 * scale_a, v1 * jnp.where(low_half, scale_a, scale_b), v2 * scale_b], axis=1
        )
        return silu_half(scaled * gain2)

    first_col = lax.broadcasted_iota(jnp.int32, (1, 2 * C2), 1) < C2

    def second_products(at_f, spans, even_rows, odd_rows, held):
        def window(refs, stop):
            parts = []
            for lo, hi in spans:
                pieces = [ref[at_f, lo + down : hi + down, 0:stop] for down in (0, 1) for ref in refs]
                parts.append(jnp.concatenate(pieces, axis=-1).reshape(-1, 4 * C1))
            return jnp.concatenate(parts, axis=0)

        for rows, refs, y2, stop in (
            (even_rows, (a_r1p, a_r0), held[0], WIDE),
            (odd_rows, (a_r0, a_r1c), held[1], PATCH_COLS),
        ):
            y2[0:rows] = lax.dot_general(
                window(refs, stop), w2[...], (((1,), (1,)), ((), ())), preferred_element_type=F32
            )

    def second_finish(f, i, at, held):
        for par in range(2):
            row = 2 * i + par
            cols = slice(par * 384, (par + 1) * 384)
            ve = held[0][at * WIDE : at * WIDE + 88, cols] + bias2
            vo = held[1][at * PATCH_COLS : (at + 1) * PATCH_COLS, cols] + bias2
            act = norm_pair(ve)
            act_o = norm_pair(vo)
            if row == 0:
                act, act_o = act * keep_top, act_o * keep_top
            if row == 9:
                act, act_o = act * keep_bottom, act_o * keep_bottom
            act = jnp.concatenate(
                [act[:8] * out_left, act[8:PATCH_COLS], act[PATCH_COLS:] * out_right], axis=0
            )
            fe[f + 2, row] = act[:PATCH_COLS].astype(BF)
            fe1[f + 2, row] = pltpu.roll(act, 87, 0)[:PATCH_COLS].astype(BF)
            fo[f + 2, row] = act_o.astype(BF)
            if 1 <= row <= 8:
                ve1 = pltpu.roll(ve, 87, 0)[:PATCH_COLS]
                ue[f, row - 1] = jnp.where(first_col, vo, ve[:PATCH_COLS]).astype(BF)
                uo[f, row - 1] = jnp.where(first_col, ve1, vo).astype(BF)

    def second(f):
        held = ((y2e, y2o), (y1a, y1b))[f % 2]
        second_products(f, ((0, 2), (3, 5)), 4 * WIDE, 4 * PATCH_COLS, held)
        for at, i in enumerate((0, 1, 3, 4)):
            second_finish(f, i, at, held)

    each_frame(inner_windows)
    first(2)
    first(3)
    second_products(slice(0, 4), ((2, 3),), 4 * WIDE, 4 * PATCH_COLS, (y2e, y2o))
    for f in range(4):
        second_finish(f, 2, f, (y2e, y2o))

    @pl.when(top)
    def _():
        tok[:, 0] = jnp.zeros((4, TOK, 4 * C0), BF)
        lat[:, 0:2] = jnp.zeros((2, 2, TOK, 2 * C0), BF)
        cf_edge[0] = jnp.zeros((2, C2, FEAT), BF)

    @pl.when(jnp.logical_not(top))
    def _():
        for copy in to_down[:3]:
            copy.wait_recv()

    @pl.when(bottom)
    def _():
        tok[:, 3] = jnp.zeros((4, TOK, 4 * C0), BF)
        lat[:, 6:8] = jnp.zeros((2, 2, TOK, 2 * C0), BF)
        cf_edge[1] = jnp.zeros((2, C2, FEAT), BF)

    @pl.when(jnp.logical_not(bottom))
    def _():
        for copy in to_up[:3]:
            copy.wait_recv()

    for t in range(2):
        all_windows(t, cached_rows, 0)
    for t in range(4):
        all_windows(t, token_rows, 2)
    for row in (0, 1, 4, 5):
        first(row)

    def third(f, start, n, acc):
        at = slice(start, start + n)
        for y in (0, 4):
            parts = []
            for dt in range(3):
                for dr in range(3):
                    rows = slice(y + dr, y + dr + 4)
                    e, o, e1 = fe[f + dt, rows, at], fo[f + dt, rows, at], fe1[f + dt, rows, at]
                    parts.append(
                        jnp.concatenate(
                            [jnp.concatenate([e, o], axis=2), jnp.concatenate([o, e1], axis=2)],
                            axis=0,
                        ).reshape(8 * n, 768)
                    )
            mine = slice(y, y + 4)
            parts.append(
                jnp.concatenate([ue[f, mine, at], uo[f, mine, at]], axis=0).reshape(8 * n, 384)
            )
            res = jnp.dot(jnp.concatenate(parts, axis=1), w3[...], preferred_element_type=F32)
            both = jnp.concatenate([res[: 4 * n], res[4 * n :]], axis=1)
            for piece in range(3):
                acc[piece, y * n : (y + 4) * n, :] = both[:, piece * 128 : (piece + 1) * 128]
        for s in range(n):
            part = pl.ds(s, 8, stride=n)
            x = jnp.concatenate([acc[piece, part, :] for piece in range(3)], axis=1) + bias3
            ostage[f, :, (start + s) * 384 : (start + s + 1) * 384] = x.astype(BF)

    for f in range(3):
        second(f)

    @pl.when(jnp.logical_not(top))
    def _():
        to_down[3].wait_recv()

    @pl.when(jnp.logical_not(bottom))
    def _():
        to_up[3].wait_recv()

    for t in range(2):
        cached_row(t, 0, cf_edge[0, t])
        cached_row(t, 9, cf_edge[1, t])

    half_lanes = PATCH_COLS * 384
    lanes = pl.ds(pl.multiple_of(ta * half_lanes, 128), half_lanes)

    def sent(slot, k, start, n):
        f = 2 * other + k
        there = pl.ds(pl.multiple_of(ta * half_lanes + start * 384, 128), n * 384)
        return remote(
            slot,
            ostage.at[f, :, start * 384 : (start + n) * 384],
            out.at[k, :, there],
            (other, ha),
        )

    sends = [sent(9, 0, 0, 48), sent(10, 0, 48, 32), sent(11, 1, 0, PATCH_COLS)]

    def kept(k):
        f = 2 * ta + k
        return pltpu.make_async_copy(ostage.at[f], out.at[k, :, lanes], local_sem.at[6 + k])

    third(2 * other, 0, 48, acc_a)
    sends[0].start()
    third(2 * other, 48, 32, acc_b)
    sends[1].start()
    second(3)
    third(2 * other + 1, 0, PATCH_COLS, acc_a)
    sends[2].start()
    third(2 * ta, 0, PATCH_COLS, acc_b)
    kept(0).start()
    third(2 * ta + 1, 0, PATCH_COLS, acc_a)
    kept(1).start()
    beside.wait_send()

    @pl.when(jnp.logical_not(top))
    def _():
        for copy in to_up:
            copy.wait_send()

    @pl.when(jnp.logical_not(bottom))
    def _():
        for copy in to_down:
            copy.wait_send()

    for k in range(2):
        kept(k).wait()
    for copy in sends:
        copy.wait()


def copied(x):
    def body(src, dst, buf, sem_in, sem_out):
        size = 15360
        into, back = [], []
        for k in range(2):
            for n in range(4):
                at = slice(n * size, (n + 1) * size)
                into.append(pltpu.make_async_copy(src.at[k, :, at], buf.at[k, :, at], sem_in.at[k, n]))
                back.append(pltpu.make_async_copy(buf.at[k, :, at], dst.at[k, :, at], sem_out.at[k, n]))
        for copy in into:
            copy.start()
        for copy, after in zip(into, back):
            copy.wait()
            after.start()
        for copy in back:
            copy.wait()

    spec = pl.BlockSpec(memory_space=pl.ANY)
    return pl.pallas_call(
        body,
        out_shape=jax.ShapeDtypeStruct(x.shape, x.dtype),
        in_specs=[spec],
        out_specs=spec,
        scratch_shapes=[
            pltpu.VMEM(x.shape, BF),
            pltpu.SemaphoreType.DMA((2, 4)),
            pltpu.SemaphoreType.DMA((2, 4)),
        ],
    )(x)


def shards(
    tokens,
    cache_latent,
    cache_feature,
    weight_in,
    weight_up,
    weight_out,
    weight_skip,
    bias_in,
    bias_up,
    bias_out,
    gain_in,
    gain_up,
):
    tok = tokens.reshape(4, 2, PATCH_COLS, 4 * C0)
    lat = cache_latent.reshape(2, 4, 160, 2 * C0)
    any_spec = pl.BlockSpec(memory_space=pl.ANY)
    vmem = pl.BlockSpec(memory_space=pltpu.VMEM)
    scratch = [
        pltpu.VMEM((4, 4, TOK, 4 * C0), BF),
        pltpu.VMEM((2, 8, TOK, 2 * C0), BF),
        pltpu.VMEM((6, 4, WIDE, 256), BF),
        pltpu.VMEM((4 * WIDE, 2 * C1), F32),
        pltpu.VMEM((4 * WIDE, 2 * C1), F32),
        pltpu.VMEM((4, 6, WIDE, C1), BF),
        pltpu.VMEM((4, 6, WIDE, C1), BF),
        pltpu.VMEM((4, 6, PATCH_COLS, C1), BF),
        pltpu.VMEM((4 * WIDE, 4 * C2), F32),
        pltpu.VMEM((4 * PATCH_COLS, 4 * C2), F32),
        pltpu.VMEM((6, 10, PATCH_COLS, 2 * C2), BF),
        pltpu.VMEM((6, 10, PATCH_COLS, 2 * C2), BF),
        pltpu.VMEM((6, 10, PATCH_COLS, 2 * C2), BF),
        pltpu.VMEM((4, 8, PATCH_COLS, 2 * C2), BF),
        pltpu.VMEM((4, 8, PATCH_COLS, 2 * C2), BF),
        pltpu.VMEM((2, 8, C2, FEAT), BF),
        pltpu.VMEM((2, 2, C2, FEAT), BF),
        pltpu.VMEM((6 * PATCH_COLS, FEAT), BF),
        pltpu.VMEM((3, 8 * PATCH_COLS, 128), F32),
        pltpu.VMEM((3, 8 * PATCH_COLS, 128), F32),
        pltpu.VMEM((4, 8, PATCH_COLS * 384), BF),
        pltpu.VMEM((3, 3, 3, C0, C1), BF),
        pltpu.VMEM((3, 3, C2, C1), BF),
        pltpu.VMEM((9, 3 * C2, C3), BF),
        pltpu.VMEM((2, 768, 2 * C1), BF),
        pltpu.VMEM((4 * C2, 4 * C1), BF),
        pltpu.VMEM((9 * 768 + 384, 2 * C3), BF),
        pltpu.SemaphoreType.DMA((12,)),
        pltpu.SemaphoreType.DMA((12,)),
        pltpu.SemaphoreType.DMA((8,)),
    ]
    return copied(pl.pallas_call(
        kernel,
        out_shape=jax.ShapeDtypeStruct((2, 8, 640 * C3), BF),
        in_specs=[any_spec] * 6 + [vmem] * 6,
        out_specs=any_spec,
        scratch_shapes=scratch,
        compiler_params=pltpu.CompilerParams(
            collective_id=0, has_side_effects=True, vmem_limit_bytes=52 * 1024 * 1024
        ),
        cost_estimate=pl.CostEstimate(
            flops=28_000_000_000, bytes_accessed=16_000_000, transcendentals=5_000_000
        ),
    )(
        tok,
        lat,
        cache_feature.transpose(0, 1, 3, 2),
        weight_in,
        weight_up.transpose(0, 1, 3, 2),
        weight_out.reshape(9, 3 * C2, C3),
        weight_skip,
        bias_in,
        bias_up,
        bias_out,
        gain_in,
        gain_up,
    ))


def solution(mesh):
    placed = (
        P(None, "ha", "ta"),
        P(None, "ha", None),
        P(None, "ha", None, None),
        P(),
        P(),
        P(),
        P(),
        P(),
        P(),
        P(),
        P(),
        P(),
    )
    return jax.shard_map(
        shards, mesh=mesh, in_specs=placed, out_specs=P("ta", "ha", None), check_vma=False
    )
```

```python
import functools

import jax
import jax.numpy as jnp
from jax import lax
from jax.experimental import pallas as pl
from jax.experimental.pallas import tpu as pltpu
from jax.sharding import PartitionSpec as P

C0 = 16
C1 = 384
C2 = 192
C3 = 96
FRAMES = 4
PATCH_COLS = 80
HALO = 16
TOK = PATCH_COLS + 2 * HALO
WIDE = 96
FEAT = 384
BF = jnp.bfloat16
F32 = jnp.float32
MESH = pl.DeviceIdType.MESH


def silu_half(half):
    return half + half * jnp.tanh(half)


def kernel(
    tokens,
    cache_lat,
    cache_feat,
    w_in_hbm,
    w_up_hbm,
    w_out_hbm,
    w_skip,
    b1,
    b2,
    b3,
    g1,
    g2,
    out,
    tok,
    lat,
    win,
    y1a,
    y1b,
    a_r0,
    a_r1p,
    a_r1c,
    y2e,
    y2o,
    fe,
    fo,
    fe1,
    ue,
    uo,
    cf,
    cf_edge,
    pick,
    acc_a,
    acc_b,
    ostage,
    w_in,
    w_up,
    w_out,
    w1,
    w2,
    w3,
    send_sem,
    recv_sem,
    local_sem,
):
    ta = lax.axis_index("ta")
    ha = lax.axis_index("ha")
    n_ha = lax.axis_size("ha")
    up = jnp.maximum(ha - 1, 0)
    down = jnp.minimum(ha + 1, n_ha - 1)
    other = 1 - ta
    top = ha == 0
    bottom = ha == n_ha - 1
    left = ta == 0

    lat_src = pl.multiple_of(ta * 64, 16)
    lat_dst = pl.multiple_of(HALO - ta * HALO, 16)
    feat = pl.ds(pl.multiple_of(ta * 256, 128), 384)
    edge_src = pl.multiple_of((1 - ta) * 64, 16)
    edge_dst = pl.multiple_of(ta * 96, 16)
    local = [
        pltpu.make_async_copy(
            tokens, tok.at[:, 1:3, HALO : HALO + PATCH_COLS], local_sem.at[0]
        ),
        pltpu.make_async_copy(
            cache_lat.at[:, :, pl.ds(lat_src, 96)],
            lat.at[:, 2:6, pl.ds(lat_dst, 96)],
            local_sem.at[1],
        ),
        pltpu.make_async_copy(w_in_hbm, w_in, local_sem.at[2]),
        pltpu.make_async_copy(w_up_hbm, w_up, local_sem.at[3]),
        pltpu.make_async_copy(cache_feat.at[:, :, :, feat], cf, local_sem.at[4]),
        pltpu.make_async_copy(w_out_hbm, w_out, local_sem.at[5]),
    ]
    for copy in local:
        copy.start()

    barrier = pltpu.get_barrier_semaphore()

    def hello(partner):
        pl.semaphore_signal(barrier, inc=1, device_id=partner, device_id_type=MESH)

    hello((other, ha))

    @pl.when(jnp.logical_not(top))
    def _():
        hello((ta, up))
        hello((other, up))

    @pl.when(jnp.logical_not(bottom))
    def _():
        hello((ta, down))
        hello((other, down))

    def remote(slot, src, dst, to):
        return pltpu.make_async_remote_copy(
            src_ref=src,
            dst_ref=dst,
            send_sem=send_sem.at[slot],
            recv_sem=recv_sem.at[slot],
            device_id=to,
            device_id_type=MESH,
        )

    own = slice(HALO, HALO + PATCH_COLS)
    to_up = [
        remote(0, tokens.at[:, 0], tok.at[:, 3, own], (ta, up)),
        remote(
            1,
            tokens.at[:, 0, pl.ds(edge_src, HALO)],
            tok.at[:, 3, pl.ds(edge_dst, HALO)],
            (other, up),
        ),
        remote(
            2,
            cache_lat.at[:, 0:2, pl.ds(lat_src, 96)],
            lat.at[:, 6:8, pl.ds(lat_dst, 96)],
            (ta, up),
        ),
        remote(3, cache_feat.at[:, 0, :, feat], cf_edge.at[1], (ta, up)),
    ]
    to_down = [
        remote(4, tokens.at[:, 1], tok.at[:, 0, own], (ta, down)),
        remote(
            5,
            tokens.at[:, 1, pl.ds(edge_src, HALO)],
            tok.at[:, 0, pl.ds(edge_dst, HALO)],
            (other, down),
        ),
        remote(
            6,
            cache_lat.at[:, 2:4, pl.ds(lat_src, 96)],
            lat.at[:, 0:2, pl.ds(lat_dst, 96)],
            (ta, down),
        ),
        remote(7, cache_feat.at[:, 7, :, feat], cf_edge.at[0], (ta, down)),
    ]
    beside = remote(
        8,
        tokens.at[:, :, pl.ds(edge_src, HALO)],
        tok.at[:, 1:3, pl.ds(edge_dst, HALO)],
        (other, ha),
    )

    local[2].wait()

    def build_first(dt):
        for block in range(16):
            row_tap = ((block >> 1 & 1) + 2 * (block >> 2 & 1) + 1) % 4
            col_tap = ((block & 1) + 2 * (block >> 3) + 1) % 4
            for q in range(2):
                for r in range(2):
                    dr, dc = row_tap - q, col_tap - r
                    if 0 <= dr < 3 and 0 <= dc < 3:
                        piece = w_in[dt, dr, dc]
                    else:
                        piece = jnp.zeros((C0, C1), BF)
                    at = dt * 256 + block * C0
                    w1[q, at : at + C0, r * C1 : (r + 1) * C1] = piece

    for dt in range(3):
        build_first(dt)

    partners = 5 - 2 * top.astype(jnp.int32) - 2 * bottom.astype(jnp.int32)
    pl.semaphore_wait(barrier, partners)
    beside.start()

    @pl.when(jnp.logical_not(top))
    def _():
        for copy in to_up:
            copy.start()

    @pl.when(jnp.logical_not(bottom))
    def _():
        for copy in to_down:
            copy.start()

    @pl.when(left)
    def _():
        tok[:, :, 0:HALO] = jnp.zeros((4, 4, HALO, 4 * C0), BF)
        lat[:, :, 0:HALO] = jnp.zeros((2, 8, HALO, 2 * C0), BF)

    @pl.when(jnp.logical_not(left))
    def _():
        tok[:, :, HALO + PATCH_COLS :] = jnp.zeros((4, 4, HALO, 4 * C0), BF)
        lat[:, :, HALO + PATCH_COLS :] = jnp.zeros((2, 8, HALO, 2 * C0), BF)

    lane_f = lax.broadcasted_iota(jnp.int32, (PATCH_COLS, FEAT), 1)
    sub_f = lax.broadcasted_iota(jnp.int32, (PATCH_COLS, FEAT), 0)
    for b in range(6):
        hit = lane_f == 4 * sub_f + (b - 1) + 64 * ta
        pick[b * PATCH_COLS : (b + 1) * PATCH_COLS, :] = jnp.where(hit, 1.0, 0.0).astype(BF)

    local[4].wait()

    def cached_row(t, row, columns):
        res = lax.dot_general(
            pick[...], columns, (((1,), (1,)), ((), ())), preferred_element_type=F32
        )
        for b, ref in enumerate((fe, fo, fe1)):
            at = 2 * b * PATCH_COLS
            pair = jnp.concatenate(
                [res[at : at + PATCH_COLS], res[at + PATCH_COLS : at + 2 * PATCH_COLS]], axis=1
            )
            ref[t, row] = pair.astype(BF)

    for t in range(2):
        for row in range(1, 9):
            cached_row(t, row, cf[t, row - 1])

    local[3].wait()
    taps = {(0, 0): (0, 1), (1, 0): (2,), (0, 1): (0,), (1, 1): (1, 2)}

    def total(parts):
        return functools.reduce(lambda x, y: x + y, parts)

    for kr in range(2):
        for pr in range(2):
            rows = [
                total([w_up[dr, dc].astype(F32) for dr in taps[kr, pr]]) for dc in range(3)
            ]
            for kc in range(2):
                for pc in range(2):
                    out_at = (2 * pr + pc) * C2
                    in_at = (2 * kr + kc) * C1
                    w2[out_at : out_at + C2, in_at : in_at + C1] = total(
                        [rows[dc] for dc in taps[kc, pc]]
                    ).astype(BF)

    local[5].wait()

    z = jnp.zeros((C2, C3), BF)
    for n in range(9):
        w = w_out[n]
        w3[n * 768 : (n + 1) * 768, :] = jnp.concatenate(
            [jnp.concatenate([w, z], axis=0), jnp.concatenate([z, w], axis=0)], axis=1
        )
    ws = w_skip[...]
    w3[9 * 768 : 9 * 768 + C2, :] = jnp.concatenate([z, ws], axis=1)
    w3[9 * 768 + C2 :, :] = jnp.concatenate([ws, z], axis=1)

    bias1 = b1[...].reshape(1, C1)
    gain1 = 0.5 * g1[...].reshape(1, C1)
    bias2 = jnp.concatenate([b2[...].reshape(1, C2)] * 2, axis=1)
    gain2 = 0.5 * jnp.concatenate([g2[...].reshape(1, C2)] * 2, axis=1)
    bias3 = jnp.concatenate([b3[...].reshape(1, C3)] * 4, axis=1)

    beside.wait_recv()
    local[0].wait()
    local[1].wait()

    lane64 = lax.broadcasted_iota(jnp.int32, (TOK, 4 * C0), 1)
    second_row = lane64 >= 2 * C0
    second_col = (lane64 // C0) % 2 == 1

    def windows(t, rows, which):
        for u in which:
            above = rows[max(u - 1, 0)]
            below = rows[min(u + 1, 3)]
            here = rows[u]
            vert = jnp.where(second_row, above, below)
            horiz = jnp.where(second_col, pltpu.roll(here, 1, 0), pltpu.roll(here, TOK - 1, 0))
            diag = jnp.where(second_col, pltpu.roll(vert, 1, 0), pltpu.roll(vert, TOK - 1, 0))
            full = jnp.concatenate([here, vert, horiz, diag], axis=1)
            win[t, u] = pltpu.roll(full, 1, 0)[HALO : HALO + WIDE].astype(BF)

    def cached_rows(t, u):
        return jnp.concatenate(
            [lat[t, 2 * u].astype(F32), lat[t, 2 * u + 1].astype(F32)], axis=1
        )

    def token_rows(t, u):
        return tok[t, u].astype(F32)

    def inner_windows(t, get, base):
        first, last = get(t, 1), get(t, 2)
        windows(t + base, [first, first, last, last], (1, 2))

    def all_windows(t, get, base):
        windows(t + base, [get(t, u) for u in range(4)], range(4))

    keep_top = jnp.where(top, 0.0, 1.0)
    keep_bottom = jnp.where(bottom, 0.0, 1.0)
    sub8 = lax.broadcasted_iota(jnp.int32, (8, 2 * C2), 0)
    lane8 = lax.broadcasted_iota(jnp.int32, (8, 2 * C2), 1)
    not_left = jnp.where(jnp.logical_and(sub8 == 0, left), 0.0, 1.0)
    keep_right = jnp.where(left, 1.0, 0.0)
    out_left = jnp.where(
        jnp.logical_and(jnp.logical_and(sub8 == 0, lane8 < C2), left), 0.0, 1.0
    )
    out_right = jnp.where(
        jnp.logical_and(jnp.logical_and(sub8 == 0, lane8 >= C2), jnp.logical_not(left)), 0.0, 1.0
    )

    def first(row):
        u, q = (row + 1) // 2, (row + 1) % 2
        y1 = (y1a, y1b)[row % 2]
        lhs = jnp.concatenate(
            [win[dt : dt + 4, u].reshape(4 * WIDE, 256) for dt in range(3)], axis=1
        )
        y1[...] = jnp.dot(lhs, w1[q], preferred_element_type=F32)
        for f in range(4):
            acts = []
            for r in range(2):
                v = y1[f * WIDE : (f + 1) * WIDE, r * C1 : (r + 1) * C1] + bias1
                scale = lax.rsqrt(jnp.mean(v * v, axis=1, keepdims=True) + 1e-06)
                act = silu_half(v * scale * gain1)
                if row == 0:
                    act = act * keep_top
                if row == 5:
                    act = act * keep_bottom
                acts.append(act)
            shifted = pltpu.roll(acts[0], WIDE - 1, 0)
            a_r0[f, row, :PATCH_COLS] = shifted[:PATCH_COLS].astype(BF)
            a_r0[f, row, PATCH_COLS:] = (shifted[PATCH_COLS:] * keep_right).astype(BF)
            a_r1p[f, row] = jnp.concatenate([acts[1][:8] * not_left, acts[1][8:]], axis=0).astype(
                BF
            )
            a_r1c[f, row] = pltpu.roll(acts[1], WIDE - 1, 0)[:PATCH_COLS].astype(BF)

    low_half = lax.broadcasted_iota(jnp.int32, (1, 128), 1) < 64

    def norm_pair(v):
        v0, v1, v2 = v[:, 0:128], v[:, 128:256], v[:, 256:384]
        sq1 = v1 * v1
        sum_a = jnp.sum(v0 * v0 + jnp.where(low_half, sq1, 0.0), axis=1, keepdims=True)
        sum_b = jnp.sum(v2 * v2 + jnp.where(low_half, 0.0, sq1), axis=1, keepdims=True)
        scale_a = lax.rsqrt(sum_a * (1.0 / C2) + 1e-06)
        scale_b = lax.rsqrt(sum_b * (1.0 / C2) + 1e-06)
        scaled = jnp.concatenate(
            [v0 * scale_a, v1 * jnp.where(low_half, scale_a, scale_b), v2 * scale_b], axis=1
        )
        return silu_half(scaled * gain2)

    first_col = lax.broadcasted_iota(jnp.int32, (1, 2 * C2), 1) < C2

    def second_products(at_f, spans, even_rows, odd_rows, held):
        def window(refs, stop):
            parts = []
            for lo, hi in spans:
                pieces = [ref[at_f, lo + down : hi + down, 0:stop] for down in (0, 1) for ref in refs]
                parts.append(jnp.concatenate(pieces, axis=-1).reshape(-1, 4 * C1))
            return jnp.concatenate(parts, axis=0)

        for rows, refs, y2, stop in (
            (even_rows, (a_r1p, a_r0), held[0], WIDE),
            (odd_rows, (a_r0, a_r1c), held[1], PATCH_COLS),
        ):
            y2[0:rows] = lax.dot_general(
                window(refs, stop), w2[...], (((1,), (1,)), ((), ())), preferred_element_type=F32
            )

    def second_finish(f, i, at, held):
        for par in range(2):
            row = 2 * i + par
            cols = slice(par * 384, (par + 1) * 384)
            ve = held[0][at * WIDE : at * WIDE + 88, cols] + bias2
            vo = held[1][at * PATCH_COLS : (at + 1) * PATCH_COLS, cols] + bias2
            act = norm_pair(ve)
            act_o = norm_pair(vo)
            if row == 0:
                act, act_o = act * keep_top, act_o * keep_top
            if row == 9:
                act, act_o = act * keep_bottom, act_o * keep_bottom
            act = jnp.concatenate(
                [act[:8] * out_left, act[8:PATCH_COLS], act[PATCH_COLS:] * out_right], axis=0
            )
            fe[f + 2, row] = act[:PATCH_COLS].astype(BF)
            fe1[f + 2, row] = pltpu.roll(act, 87, 0)[:PATCH_COLS].astype(BF)
            fo[f + 2, row] = act_o.astype(BF)
            if 1 <= row <= 8:
                ve1 = pltpu.roll(ve, 87, 0)[:PATCH_COLS]
                ue[f, row - 1] = jnp.where(first_col, vo, ve[:PATCH_COLS]).astype(BF)
                uo[f, row - 1] = jnp.where(first_col, ve1, vo).astype(BF)

    def second(f):
        held = ((y2e, y2o), (y1a, y1b))[f % 2]
        second_products(f, ((0, 2), (3, 5)), 4 * WIDE, 4 * PATCH_COLS, held)
        for at, i in enumerate((0, 1, 3, 4)):
            second_finish(f, i, at, held)

    for t in range(2):
        inner_windows(t, cached_rows, 0)
    for t in range(4):
        inner_windows(t, token_rows, 2)
    first(2)
    first(3)
    second_products(slice(0, 4), ((2, 3),), 4 * WIDE, 4 * PATCH_COLS, (y2e, y2o))
    for f in range(4):
        second_finish(f, 2, f, (y2e, y2o))

    @pl.when(top)
    def _():
        tok[:, 0] = jnp.zeros((4, TOK, 4 * C0), BF)
        lat[:, 0:2] = jnp.zeros((2, 2, TOK, 2 * C0), BF)
        cf_edge[0] = jnp.zeros((2, C2, FEAT), BF)

    @pl.when(jnp.logical_not(top))
    def _():
        for copy in to_down[:3]:
            copy.wait_recv()

    @pl.when(bottom)
    def _():
        tok[:, 3] = jnp.zeros((4, TOK, 4 * C0), BF)
        lat[:, 6:8] = jnp.zeros((2, 2, TOK, 2 * C0), BF)
        cf_edge[1] = jnp.zeros((2, C2, FEAT), BF)

    @pl.when(jnp.logical_not(bottom))
    def _():
        for copy in to_up[:3]:
            copy.wait_recv()

    for t in range(2):
        all_windows(t, cached_rows, 0)
    for t in range(4):
        all_windows(t, token_rows, 2)
    for row in (0, 1, 4, 5):
        first(row)

    def third(f, start, n, acc):
        at = slice(start, start + n)
        for y in (0, 4):
            parts = []
            for dt in range(3):
                for dr in range(3):
                    rows = slice(y + dr, y + dr + 4)
                    e, o, e1 = fe[f + dt, rows, at], fo[f + dt, rows, at], fe1[f + dt, rows, at]
                    parts.append(
                        jnp.concatenate(
                            [jnp.concatenate([e, o], axis=2), jnp.concatenate([o, e1], axis=2)],
                            axis=0,
                        ).reshape(8 * n, 768)
                    )
            mine = slice(y, y + 4)
            parts.append(
                jnp.concatenate([ue[f, mine, at], uo[f, mine, at]], axis=0).reshape(8 * n, 384)
            )
            res = jnp.dot(jnp.concatenate(parts, axis=1), w3[...], preferred_element_type=F32)
            both = jnp.concatenate([res[: 4 * n], res[4 * n :]], axis=1)
            for piece in range(3):
                acc[piece, y * n : (y + 4) * n, :] = both[:, piece * 128 : (piece + 1) * 128]
        for s in range(n):
            part = pl.ds(s, 8, stride=n)
            x = jnp.concatenate([acc[piece, part, :] for piece in range(3)], axis=1) + bias3
            ostage[f, :, (start + s) * 384 : (start + s + 1) * 384] = x.astype(BF)

    for f in range(3):
        second(f)

    @pl.when(jnp.logical_not(top))
    def _():
        to_down[3].wait_recv()

    @pl.when(jnp.logical_not(bottom))
    def _():
        to_up[3].wait_recv()

    for t in range(2):
        cached_row(t, 0, cf_edge[0, t])
        cached_row(t, 9, cf_edge[1, t])

    half_lanes = PATCH_COLS * 384
    lanes = pl.ds(pl.multiple_of(ta * half_lanes, 128), half_lanes)

    def sent(slot, k, start, n):
        f = 2 * other + k
        there = pl.ds(pl.multiple_of(ta * half_lanes + start * 384, 128), n * 384)
        return remote(
            slot,
            ostage.at[f, :, start * 384 : (start + n) * 384],
            out.at[k, :, there],
            (other, ha),
        )

    sends = [sent(9, 0, 0, 48), sent(10, 0, 48, 32), sent(11, 1, 0, PATCH_COLS)]

    def kept(k):
        f = 2 * ta + k
        return pltpu.make_async_copy(ostage.at[f], out.at[k, :, lanes], local_sem.at[6 + k])

    third(2 * other, 0, 48, acc_a)
    sends[0].start()
    third(2 * other, 48, 32, acc_b)
    sends[1].start()
    second(3)
    third(2 * other + 1, 0, PATCH_COLS, acc_a)
    sends[2].start()
    third(2 * ta, 0, PATCH_COLS, acc_b)
    kept(0).start()
    third(2 * ta + 1, 0, PATCH_COLS, acc_a)
    kept(1).start()
    beside.wait_send()

    @pl.when(jnp.logical_not(top))
    def _():
        for copy in to_up:
            copy.wait_send()

    @pl.when(jnp.logical_not(bottom))
    def _():
        for copy in to_down:
            copy.wait_send()

    for k in range(2):
        kept(k).wait()
    for copy in sends:
        copy.wait()


def copied(x):
    def body(src, dst, buf, sem_in, sem_out):
        size = 15360
        into, back = [], []
        for k in range(2):
            for n in range(4):
                at = slice(n * size, (n + 1) * size)
                into.append(pltpu.make_async_copy(src.at[k, :, at], buf.at[k, :, at], sem_in.at[k, n]))
                back.append(pltpu.make_async_copy(buf.at[k, :, at], dst.at[k, :, at], sem_out.at[k, n]))
        for copy in into:
            copy.start()
        for copy, after in zip(into, back):
            copy.wait()
            after.start()
        for copy in back:
            copy.wait()

    spec = pl.BlockSpec(memory_space=pl.ANY)
    return pl.pallas_call(
        body,
        out_shape=jax.ShapeDtypeStruct(x.shape, x.dtype),
        in_specs=[spec],
        out_specs=spec,
        scratch_shapes=[
            pltpu.VMEM(x.shape, BF),
            pltpu.SemaphoreType.DMA((2, 4)),
            pltpu.SemaphoreType.DMA((2, 4)),
        ],
    )(x)


def shards(
    tokens,
    cache_latent,
    cache_feature,
    weight_in,
    weight_up,
    weight_out,
    weight_skip,
    bias_in,
    bias_up,
    bias_out,
    gain_in,
    gain_up,
):
    tok = tokens.reshape(4, 2, PATCH_COLS, 4 * C0)
    lat = cache_latent.reshape(2, 4, 160, 2 * C0)
    any_spec = pl.BlockSpec(memory_space=pl.ANY)
    vmem = pl.BlockSpec(memory_space=pltpu.VMEM)
    scratch = [
        pltpu.VMEM((4, 4, TOK, 4 * C0), BF),
        pltpu.VMEM((2, 8, TOK, 2 * C0), BF),
        pltpu.VMEM((6, 4, WIDE, 256), BF),
        pltpu.VMEM((4 * WIDE, 2 * C1), F32),
        pltpu.VMEM((4 * WIDE, 2 * C1), F32),
        pltpu.VMEM((4, 6, WIDE, C1), BF),
        pltpu.VMEM((4, 6, WIDE, C1), BF),
        pltpu.VMEM((4, 6, PATCH_COLS, C1), BF),
        pltpu.VMEM((4 * WIDE, 4 * C2), F32),
        pltpu.VMEM((4 * PATCH_COLS, 4 * C2), F32),
        pltpu.VMEM((6, 10, PATCH_COLS, 2 * C2), BF),
        pltpu.VMEM((6, 10, PATCH_COLS, 2 * C2), BF),
        pltpu.VMEM((6, 10, PATCH_COLS, 2 * C2), BF),
        pltpu.VMEM((4, 8, PATCH_COLS, 2 * C2), BF),
        pltpu.VMEM((4, 8, PATCH_COLS, 2 * C2), BF),
        pltpu.VMEM((2, 8, C2, FEAT), BF),
        pltpu.VMEM((2, 2, C2, FEAT), BF),
        pltpu.VMEM((6 * PATCH_COLS, FEAT), BF),
        pltpu.VMEM((3, 8 * PATCH_COLS, 128), F32),
        pltpu.VMEM((3, 8 * PATCH_COLS, 128), F32),
        pltpu.VMEM((4, 8, PATCH_COLS * 384), BF),
        pltpu.VMEM((3, 3, 3, C0, C1), BF),
        pltpu.VMEM((3, 3, C2, C1), BF),
        pltpu.VMEM((9, 3 * C2, C3), BF),
        pltpu.VMEM((2, 768, 2 * C1), BF),
        pltpu.VMEM((4 * C2, 4 * C1), BF),
        pltpu.VMEM((9 * 768 + 384, 2 * C3), BF),
        pltpu.SemaphoreType.DMA((12,)),
        pltpu.SemaphoreType.DMA((12,)),
        pltpu.SemaphoreType.DMA((8,)),
    ]
    return copied(pl.pallas_call(
        kernel,
        out_shape=jax.ShapeDtypeStruct((2, 8, 640 * C3), BF),
        in_specs=[any_spec] * 6 + [vmem] * 6,
        out_specs=any_spec,
        scratch_shapes=scratch,
        compiler_params=pltpu.CompilerParams(
            collective_id=0, has_side_effects=True, vmem_limit_bytes=52 * 1024 * 1024
        ),
        cost_estimate=pl.CostEstimate(
            flops=28_000_000_000, bytes_accessed=16_000_000, transcendentals=5_000_000
        ),
    )(
        tok,
        lat,
        cache_feature.transpose(0, 1, 3, 2),
        weight_in,
        weight_up.transpose(0, 1, 3, 2),
        weight_out.reshape(9, 3 * C2, C3),
        weight_skip,
        bias_in,
        bias_up,
        bias_out,
        gain_in,
        gain_up,
    ))


def solution(mesh):
    placed = (
        P(None, "ha", "ta"),
        P(None, "ha", None),
        P(None, "ha", None, None),
        P(),
        P(),
        P(),
        P(),
        P(),
        P(),
        P(),
        P(),
        P(),
    )
    return jax.shard_map(
        shards, mesh=mesh, in_specs=placed, out_specs=P("ta", "ha", None), check_vma=False
    )
```
